32 devices in a mesh: lat: 4 (over y, x), lon: 8 (over z, core).
Axes of the slice: x: 2, y: 2, z: 4, core: 2. Of those that a mesh axis runs over, the one named last changes fastest.
Arguments:
- prior_state: bfloat16 [2, 4, 80, 32, 1024], P(None, None, None, 'lat', 'lon'), may hold values from -6 to 6
- courant: float32 [2, 4, 32, 1024], P(None, None, 'lat', 'lon'), may hold values from -0.45 to 0.45
- obs_tile: int32 [64], replicated, may hold values from 0 to 31, as said below
- obs_site: int32 [64], replicated, may hold values from 0 to 8191
- obs_value: float32 [64], replicated, may hold values from -6 to 6
- obs_var: float32 [64], replicated, may hold values from 0.2 to 2
- loc_bits: int32 [64, 2], replicated, may hold values from 0 to 1073741823
- batch_order: int32 [4], replicated, may hold values from 0 to 3, each once
Outputs:
- analysis: bfloat16 [2, 4, 80, 32, 1024], P(None, None, None, 'lat', 'lon')
The draws below stay inside these ranges and needn't reach their ends.
Inputs may be any that keep to these rules, and one draw needn't show every extreme that they name: `obs_tile`: in each batch of 16 consecutive observations one tile owns exactly 4 observations and every other tile at most one. `loc_bits`: bits of tiles numbered 32 or more are not read.
All inputs are finite; a program needn't handle non-finite values.
Results may differ from the reference program's by a relative error of at most 0.0013.
Values may be sent and summed in bfloat16 or wider, within the bound.
No kernel may reach another device: no remote copies, remote signals or barrier semaphores. Data moves between devices by JAX's collectives and lax.ppermute only.
A program may use at most 64 MiB of HBM per device.

```python
import math
import jax
import jax.numpy as jnp
from jax import lax

FIELD_COUNT = 2
LEVEL_COUNT = 4
ENSEMBLE_SIZE = 80
TILE_LAT_ROWS = 8
TILE_LON_COLUMNS = 128
OBSERVED_BATCH = 16
BATCHES = 4
CAP = 4
NOBS = 64
WORDS = 2
NLAT = 32
NLON = 1024
N_LAT = 4
N_LON = 8
DEVICES = 32


def draw_obs_tile(key, part):
    collected = []
    for batch_index in range(BATCHES):
        subkey = jax.random.fold_in(key, 7919 + batch_index)
        key_tiles, key_shuffle = jax.random.split(subkey)
        shuffled = jax.random.permutation(key_tiles, DEVICES).astype(jnp.int32)
        crowded = jnp.full((CAP,), shuffled[0], jnp.int32)
        singles = shuffled[1:OBSERVED_BATCH - CAP + 1]
        owner_tiles = jnp.concatenate([crowded, singles])
        placing = jax.random.permutation(key_shuffle, OBSERVED_BATCH)
        collected.append(owner_tiles[placing])
    return jnp.concatenate(collected)


def place_ends(array, key, smallest, largest):
    spot = [jax.random.randint(jax.random.fold_in(key, axis), (), 0, length) for axis, length in enumerate(array.shape)]
    main_axis = array.shape.index(max(array.shape))
    beside = spot[:main_axis] + [(spot[main_axis] + 1) % array.shape[main_axis]] + spot[main_axis + 1:]
    return array.at[tuple(spot)].set(smallest).at[tuple(beside)].set(largest)


def block_scale(own_key, shape, pieces, smallest, largest):
    def one(position, blocks):
        draws = jax.random.uniform(jax.random.fold_in(jax.random.fold_in(own_key, 6), position), (blocks,), jnp.float32, smallest / len(pieces), largest / len(pieces))
        return jnp.repeat(jnp.exp(draws), shape[position] // blocks).reshape((-1,) + (1,) * (len(shape) - position - 1))

    factor_of = one(*pieces[0])
    for cut in pieces[1:]:
        factor_of = factor_of * one(*cut)
    return factor_of


def scatter_about(rng, dims, deviation, bound, cuts=(), held_as=jnp.bfloat16):
    loudness = block_scale(rng, dims, cuts, -0.22, 0.18) if cuts else 1.0
    entries = jax.random.normal(rng, dims, jnp.float32) * deviation * loudness
    return jnp.minimum(jnp.maximum(entries, -bound), bound).astype(held_as)


def setup_inputs(seed: int = 0) -> dict:
    key_list = jax.random.split(jax.random.key(seed), 9)
    prior_state = scatter_about(key_list[0], (FIELD_COUNT, LEVEL_COUNT, ENSEMBLE_SIZE, NLAT, NLON), 1.0, 6.0, ((3, 4), (4, 8)))
    courant = jnp.clip(jax.random.uniform(key_list[1], (2, LEVEL_COUNT, NLAT, NLON), jnp.float32, -0.45, 0.45) * block_scale(key_list[1], (2, LEVEL_COUNT, NLAT, NLON), ((2, 4), (3, 8)), -0.4, 0.0), -0.45, 0.45)
    obs_tile = draw_obs_tile(jax.random.fold_in(key_list[8], 71), 0)
    obs_site = place_ends(jax.random.randint(key_list[3], (NOBS,), 0, FIELD_COUNT * LEVEL_COUNT * TILE_LAT_ROWS * TILE_LON_COLUMNS), jax.random.fold_in(key_list[3], 1), 0, (FIELD_COUNT * LEVEL_COUNT * TILE_LAT_ROWS * TILE_LON_COLUMNS) - 1).astype(jnp.int32)
    obs_value = scatter_about(key_list[4], (NOBS,), 1.5, 6.0, (), jnp.float32)
    obs_var = jnp.clip(jnp.exp(jax.random.uniform(key_list[5], (NOBS,), jnp.float32, math.log(0.2), math.log(2.0))), 0.2, 2.0)
    loc_bits = place_ends(jax.random.randint(key_list[6], (NOBS, WORDS), 0, 1073741824), jax.random.fold_in(key_list[6], 1), 0, 1073741823).astype(jnp.int32)
    batch_order = jax.random.permutation(key_list[7], BATCHES).astype(jnp.int32)
    return {"prior_state": prior_state, "courant": courant, "obs_tile": obs_tile, "obs_site": obs_site, "obs_value": obs_value, "obs_var": obs_var, "loc_bits": loc_bits, "batch_order": batch_order}


EPSILON = 1e-05
HIGHEST_PRECISE = lax.Precision.HIGHEST

def upwind_transport(center_value, west, east, south, north, along_lon, along_lat):
    return center_value - jnp.maximum(along_lon, 0.0) * (center_value - west) - jnp.minimum(along_lon, 0.0) * (east - center_value) - jnp.maximum(along_lat, 0.0) * (center_value - south) - jnp.minimum(along_lat, 0.0) * (north - center_value)

def tile_bits(loc_bits, tile_ids):
    bit_words = jnp.take(loc_bits, tile_ids // 30, axis=1)
    return jnp.bitwise_and(jnp.right_shift(bit_words, (tile_ids % 30)[None, :]), 1).astype(jnp.float32)

def eakf_step(prior_row, obs_val, obs_err, member_list):
    mean_prior = jnp.mean(prior_row)
    anomaly = prior_row - mean_prior
    spread = jnp.sum(anomaly * anomaly) / (member_list - 1) + EPSILON
    post_var = spread * obs_err / (spread + obs_err)
    post_mean = post_var * (mean_prior / spread + obs_val / obs_err)
    factor = jnp.sqrt(obs_err / (spread + obs_err))
    increment = factor * anomaly + post_mean - prior_row
    weights = anomaly / ((member_list - 1) * spread)
    return (increment, weights)

def reference(prior_state, courant, obs_tile, obs_site, obs_value, obs_var, loc_bits, batch_order):
    count_of_cells = TILE_LAT_ROWS * TILE_LON_COLUMNS
    lat_total = TILE_LAT_ROWS * N_LAT
    lon_total = TILE_LON_COLUMNS * N_LON
    field_idx = obs_site // (LEVEL_COUNT * count_of_cells)
    level_position = obs_site // count_of_cells % LEVEL_COUNT
    within = obs_site % count_of_cells
    global_latitude = obs_tile // N_LON * TILE_LAT_ROWS + within // TILE_LON_COLUMNS
    global_longitude = obs_tile % N_LON * TILE_LON_COLUMNS + within % TILE_LON_COLUMNS

    def select_cells(lat_pos, lon_pos):
        inside = ((lat_pos >= 0) & (lat_pos < lat_total)).astype(jnp.float32)
        clipped = jnp.clip(lat_pos, 0, lat_total - 1)
        wrapped = lon_pos % lon_total
        values = prior_state[field_idx, level_position, :, clipped, wrapped].astype(jnp.float32)
        return values * inside[:, None]
    observed_prediction = upwind_transport(select_cells(global_latitude, global_longitude), select_cells(global_latitude, global_longitude - 1), select_cells(global_latitude, global_longitude + 1), select_cells(global_latitude - 1, global_longitude), select_cells(global_latitude + 1, global_longitude), courant[0, level_position, global_latitude, global_longitude][:, None], courant[1, level_position, global_latitude, global_longitude][:, None])
    mask_all = tile_bits(loc_bits, jnp.arange(DEVICES, dtype=jnp.int32))
    transform_list = jnp.broadcast_to(jnp.eye(ENSEMBLE_SIZE, dtype=jnp.float32), (DEVICES, ENSEMBLE_SIZE, ENSEMBLE_SIZE))
    for order_index in range(BATCHES):
        batch_offset = (batch_order[order_index] * OBSERVED_BATCH).astype(jnp.int32)
        owner_tiles = lax.dynamic_slice_in_dim(obs_tile, batch_offset, OBSERVED_BATCH)
        prediction_batch = lax.dynamic_slice_in_dim(observed_prediction, batch_offset, OBSERVED_BATCH, 0)
        obs_values = lax.dynamic_slice_in_dim(obs_value, batch_offset, OBSERVED_BATCH)
        obs_errors = lax.dynamic_slice_in_dim(obs_var, batch_offset, OBSERVED_BATCH)
        mask_batch = lax.dynamic_slice_in_dim(mask_all, batch_offset, OBSERVED_BATCH, 0)
        cross_mask = jnp.take(mask_batch, owner_tiles, axis=1)
        prior_values = jnp.einsum('yz,yzm->ym', prediction_batch, transform_list[owner_tiles], precision=HIGHEST_PRECISE)

        def advance(loop_state, inputs):
            prior_values, transform_list = loop_state
            obs_index, obs_val, obs_err, cross_row, mask_row = inputs
            increment, weights = eakf_step(prior_values[obs_index], obs_val, obs_err, ENSEMBLE_SIZE)
            projected = jnp.dot(prior_values, weights, precision=HIGHEST_PRECISE)
            prior_values = prior_values + cross_row[:, None] * projected[:, None] * increment[None, :]
            turned = jnp.einsum('tef,f->te', transform_list, weights, precision=HIGHEST_PRECISE)
            transform_list = transform_list + mask_row[:, None, None] * turned[:, :, None] * increment[None, None, :]
            return ((prior_values, transform_list), None)
        (prior_values, transform_list), _ = lax.scan(advance, (prior_values, transform_list), (jnp.arange(OBSERVED_BATCH, dtype=jnp.int32), obs_values, obs_errors, cross_mask, mask_batch))
    padded = jnp.pad(prior_state, ((0, 0), (0, 0), (0, 0), (1, 1), (0, 0)))

    def one_row(row_index):
        row_block = lax.dynamic_slice_in_dim(padded, row_index * TILE_LAT_ROWS, TILE_LAT_ROWS + 2, 3).astype(jnp.float32)
        center_value = row_block[:, :, :, 1:-1]
        southern_neighbors = row_block[:, :, :, :-2]
        northern_neighbors = row_block[:, :, :, 2:]
        western_neighbors = jnp.roll(center_value, 1, axis=4)
        eastern_neighbors = jnp.roll(center_value, -1, axis=4)
        wind_per_row = lax.dynamic_slice_in_dim(courant, row_index * TILE_LAT_ROWS, TILE_LAT_ROWS, 2)
        prediction = upwind_transport(center_value, western_neighbors, eastern_neighbors, southern_neighbors, northern_neighbors, wind_per_row[0][None, :, None], wind_per_row[1][None, :, None])
        rows_per_tile = prediction.reshape(FIELD_COUNT, LEVEL_COUNT, ENSEMBLE_SIZE, TILE_LAT_ROWS, N_LON, TILE_LON_COLUMNS)
        row_transforms = lax.dynamic_slice_in_dim(transform_list, row_index * N_LON, N_LON, 0)
        result = jnp.einsum('flesnc,neg->flgsnc', rows_per_tile, row_transforms, precision=HIGHEST_PRECISE)
        return result.reshape(FIELD_COUNT, LEVEL_COUNT, ENSEMBLE_SIZE, TILE_LAT_ROWS, lon_total).astype(jnp.bfloat16)
    row_results = lax.map(one_row, jnp.arange(N_LAT, dtype=jnp.int32))
    return jnp.moveaxis(row_results, 0, 3).reshape(FIELD_COUNT, LEVEL_COUNT, ENSEMBLE_SIZE, lat_total, lon_total)
```

```python
import functools

import jax
import jax.numpy as jnp
from jax import lax
from jax.experimental import pallas as pl
from jax.experimental.pallas import tpu as pltpu
from jax.sharding import PartitionSpec as P

EPSILON = 1e-05
HIGHEST = lax.Precision.HIGHEST
LANES = 128
SUBLANES = 8
F32 = jnp.float32
BF16 = jnp.bfloat16
VMEM = pl.BlockSpec(memory_space=pltpu.VMEM)
SMEM = pl.BlockSpec(memory_space=pltpu.SMEM)
HBM = pl.BlockSpec(memory_space=pl.ANY)
PARAMS = pltpu.CompilerParams(vmem_limit_bytes=48 * 1024 * 1024)


def iota(shape, dim):
    return lax.broadcasted_iota(jnp.int32, shape, dim)


def in_order(row, order_ref):
    nobs = row.shape[1]
    batches = order_ref.shape[0]
    batch = nobs // batches
    wide = jnp.concatenate([row, jnp.zeros((1, LANES - nobs), row.dtype)], axis=1)
    wide = jnp.broadcast_to(wide, (SUBLANES, LANES))
    lane = iota((SUBLANES, LANES), 1)
    result = jnp.zeros_like(wide)
    for i in range(batches):
        moved = pltpu.roll(wide, lax.rem(i * batch - order_ref[i] * batch + LANES, LANES), 1)
        result = jnp.where(lane // batch == i, moved, result)
    return result


def observe_kernel(n_lat, n_lon, levels, x_ref, courant_ref, tile_ref, site_ref, order_ref, pay_ref):
    planes, depth, cols = x_ref.shape
    rows = courant_ref.shape[0] // (2 * levels)
    members = depth // rows
    nobs = tile_ref.shape[1]
    cells = rows * cols
    my_lat, my_lon = lax.axis_index("lat"), lax.axis_index("lon")
    me = my_lat * n_lon + my_lon

    tile = in_order(tile_ref[...], order_ref)
    site = in_order(site_ref[...], order_ref)
    tile = tile + pltpu.roll(tile, nobs, 1)
    site = site + pltpu.roll(site, nobs, 1)
    shape = (SUBLANES, LANES)
    lane = iota(shape, 1)
    sub = iota(shape, 0)
    first = lane < nobs
    plane = site // cells
    row = (site // cols) % rows
    col = site % cols
    level = plane % levels
    lat, lon = tile // n_lon, tile % n_lon
    owner = tile == me
    from_west = (lat == my_lat) & ((lon + n_lon - 1) % n_lon == my_lon) & (col == 0)
    from_east = (lat == my_lat) & ((lon + 1) % n_lon == my_lon) & (col == cols - 1)
    from_south = (lat - 1 == my_lat) & (lon == my_lon) & (row == 0)
    from_north = (lat + 1 == my_lat) & (lon == my_lon) & (row == rows - 1)
    beside = from_west | from_east
    above = from_south | from_north
    far_col = jnp.where(from_west, cols - 1, jnp.where(from_east, 0, jnp.where(above, col, -1)))
    far_row = jnp.where(from_south, rows - 1, jnp.where(from_north, 0, row))

    down = iota((cols, LANES), 0)
    picked = jnp.dot(
        courant_ref[...], (down == col[:1]).astype(F32), precision=HIGHEST, preferred_element_type=F32
    )
    which = iota((2 * levels * rows, LANES), 0)
    at_cell = (level * rows + row)[:1]
    cu = jnp.sum(jnp.where(which == at_cell, picked, 0.0), axis=0, keepdims=True)
    cv = jnp.sum(jnp.where(which == at_cell + levels * rows, picked, 0.0), axis=0, keepdims=True)
    west, east = jnp.maximum(cu, 0.0), -jnp.minimum(cu, 0.0)
    south, north = jnp.maximum(cv, 0.0), -jnp.minimum(cv, 0.0)
    centre = 1.0 - west - east - south - north

    zero = jnp.zeros(shape, F32)
    own_rows = jnp.where(sub == row, centre, zero)
    own_rows = jnp.where(sub == row - 1, south, own_rows)
    own_rows = jnp.where(sub == row + 1, north, own_rows)
    half0 = jnp.where(first, own_rows, jnp.where(sub == row, west, zero))
    half0 = jnp.where(owner, half0, zero)
    half1 = jnp.where(first, jnp.where(owner & (sub == row), east, zero), ((beside | above) & (sub == far_row)).astype(F32))
    pick0 = (down == jnp.where(first, col, col - 1)[:1]).astype(F32)
    pick1 = (down == jnp.where(first, col + 1, far_col)[:1]).astype(F32)
    picks = jnp.concatenate([pick0, pick1], axis=1).astype(BF16)
    weights = [
        jnp.concatenate([jnp.where(plane == p, half0, zero), jnp.where(plane == p, half1, zero)], axis=1)
        for p in range(planes)
    ]
    parts = []
    group = SUBLANES * rows
    for g in range(members // SUBLANES):
        block = x_ref[:, g * group : (g + 1) * group, :].reshape(planes * group, cols)
        values = jnp.dot(block, picks, preferred_element_type=F32).reshape(planes, SUBLANES, rows, 2 * LANES)
        total = values[0] * weights[0][None]
        for p in range(1, planes):
            total = total + values[p] * weights[p][None]
        parts.append(jnp.sum(total, axis=1))
    both = jnp.concatenate(parts, axis=0)
    low, high = both[:, :LANES], both[:, LANES:]
    lane_m = iota((members, LANES), 1)
    own = low + pltpu.roll(low, nobs, 1) + high
    along_lon = jnp.where(beside[:1], high, 0.0)
    along_lat = jnp.where(above[:1] & (lane_m >= nobs), high, 0.0)
    pay_ref[0:members, :] = jnp.where(lane_m < nobs, own, along_lon)
    half = members // 2
    pay_ref[members : members + half, :] = pltpu.roll(along_lat[:half], nobs, 1) + along_lat[half:]
    factor_lon = jnp.where(col == 0, west, jnp.where(col == cols - 1, east, zero))
    factor_lat = jnp.where(row == 0, south, jnp.where(row == rows - 1, north, zero))
    pay_ref[members + half :, :] = jnp.where(owner, jnp.where(first, factor_lon, factor_lat), zero)


def edges_kernel(rows, x_ref, south_ref, north_ref, west_ref, east_ref, wide_ref):
    planes, depth, cols = x_ref.shape
    members = depth // rows
    lane = iota((rows, LANES), 1)

    @pl.loop(0, planes)
    def _(p):
        west = jnp.zeros((rows, LANES), F32)
        east = jnp.zeros((rows, LANES), F32)
        block = x_ref[p].astype(F32)
        wide_ref[...] = block
        for e in range(members):
            cell = block[e * rows : (e + 1) * rows]
            west = jnp.where(lane == e, pltpu.roll(cell, e, 1) if e else cell, west)
            east = jnp.where(lane == e, pltpu.roll(cell, (e + 1) % LANES, 1), east)
        west_ref[p] = west
        east_ref[p] = east
        south_ref[p] = wide_ref[pl.ds(0, members, stride=rows), :].astype(BF16)
        north_ref[p] = wide_ref[pl.ds(rows - 1, members, stride=rows), :].astype(BF16)


def forecast_kernel(levels, x_ref, courant_ref, south_ref, north_ref, west_ref, east_ref, hi_ref, lo_ref, wide_ref, rows_ref):
    planes, depth, cols = x_ref.shape
    rows = courant_ref.shape[0] // (2 * levels)
    members = depth // rows
    lane = iota((rows, cols), 1)
    sub = iota((rows, cols), 0)

    @pl.loop(0, planes)
    def _(p):
        level = lax.rem(p, levels)
        cu = courant_ref[pl.ds(pl.multiple_of(level * rows, rows), rows), :]
        cv = courant_ref[pl.ds(pl.multiple_of((levels + level) * rows, rows), rows), :]
        west, east = jnp.maximum(cu, 0.0), -jnp.minimum(cu, 0.0)
        south, north = jnp.maximum(cv, 0.0), -jnp.minimum(cv, 0.0)
        centre = 1.0 - west - east - south - north
        rows_ref[0] = south_ref[p].astype(F32)
        rows_ref[1] = north_ref[p].astype(F32)
        halo_west = west_ref[p]
        halo_east = east_ref[p]
        for e in range(members):
            x = x_ref[p, e * rows : (e + 1) * rows, :].astype(F32)
            xw = jnp.where(lane == 0, pltpu.roll(halo_west, (LANES - e) % LANES, 1) if e else halo_west, pltpu.roll(x, 1, 1))
            xe = jnp.where(lane == cols - 1, pltpu.roll(halo_east, (cols - 1 - e) % LANES, 1), pltpu.roll(x, cols - 1, 1))
            xs = jnp.where(sub == 0, rows_ref[0, e : e + 1, :], pltpu.roll(x, 1, 0))
            xn = jnp.where(sub == rows - 1, rows_ref[1, e : e + 1, :], pltpu.roll(x, rows - 1, 0))
            wide_ref[e * rows : (e + 1) * rows, :] = centre * x + west * xw + east * xe + south * xs + north * xn
        for r in range(rows):
            f = wide_ref[pl.ds(r, members, stride=rows), :]
            hi = f.astype(BF16)
            hi_ref[p, :, r * cols : (r + 1) * cols] = hi
            lo_ref[p, :, r * cols : (r + 1) * cols] = (f - hi.astype(F32)).astype(BF16)


def tile_mask(bits, tiles):
    words = bits.shape[1]
    word = tiles // 30
    place = tiles % 30
    chosen = jnp.zeros((bits.shape[0], LANES), jnp.int32)
    for w in range(words):
        chosen = jnp.where(word == w, bits[:, w : w + 1], chosen)
    return (jnp.right_shift(chosen, place) & 1).astype(F32)


def analysis_kernel(
    n_lon,
    rows,
    order_ref,
    value_ref,
    var_ref,
    pay_ref,
    tile_ref,
    bits_ref,
    hi_hbm,
    lo_hbm,
    out_hbm,
    hi_ref,
    lo_ref,
    out_ref,
    wide_ref,
    alpha_ref,
    anomaly_ref,
    in_sem,
    out_sem,
):
    planes, members, width = hi_ref.shape
    cols = width // rows
    nobs = tile_ref.shape[1]
    batches = order_ref.shape[0]
    batch = nobs // batches
    blocks = nobs // SUBLANES
    fetch_hi = pltpu.make_async_copy(hi_hbm, hi_ref, in_sem.at[0])
    fetch_lo = pltpu.make_async_copy(lo_hbm, lo_ref, in_sem.at[1])
    fetch_hi.start()
    fetch_lo.start()

    me = lax.axis_index("lat") * n_lon + lax.axis_index("lon")
    tile = in_order(tile_ref[...], order_ref)
    bits = jnp.concatenate(
        [bits_ref[pl.ds(pl.multiple_of(order_ref[i] * batch, batch), batch), :] for i in range(batches)], axis=0
    )
    mask = tile_mask(bits, tile[:1])
    mine = tile_mask(bits, jnp.full((1, LANES), me, jnp.int32))
    square = jnp.concatenate([mask, jnp.zeros((LANES - nobs, LANES), F32)], axis=0)
    turned = square.T

    half = members // 2
    own_lon = pay_ref[0:members, :]
    folded = pay_ref[members : members + half, :]
    factors = pay_ref[members + half : members + half + 1, :]
    first = iota((members, LANES), 1) < nobs
    along_lat = jnp.concatenate([folded, pltpu.roll(folded, nobs, 1)], axis=0)
    prior = own_lon + factors * pltpu.roll(own_lon, nobs, 1) + pltpu.roll(factors, nobs, 1) * along_lat
    prior = jnp.where(first, prior, 0.0)
    mean = jnp.sum(prior, axis=0, keepdims=True) * (1.0 / members)
    spread = prior - mean
    gram = lax.dot_general(spread, spread, (((0,), (0,)), ((), ())), precision=HIGHEST, preferred_element_type=F32)
    tall = jnp.concatenate([spread, jnp.zeros((LANES - members, LANES), F32)], axis=0).T

    def cut(array):
        return [array[b * SUBLANES : (b + 1) * SUBLANES] for b in range(blocks)]

    c_rows, b_rows, a_rows = cut(gram), cut(tall), cut(tall)
    masks, mines, turns = cut(mask), cut(mine), cut(turned)
    mean_own = jnp.zeros((1, LANES), F32)
    inv = 1.0 / (members - 1)
    for k in range(nobs):
        b, s = divmod(k, SUBLANES)
        at = order_ref[k // batch] * batch + k % batch
        r = jnp.full((1, 1), var_ref[at], F32)
        o = jnp.full((1, 1), value_ref[at], F32)
        g_c, g_b, g_a = (block[b][s : s + 1] for block in (c_rows, b_rows, a_rows))
        g_kk = g_c[:, k : k + 1]
        m_k = mean[:, k : k + 1]
        v = g_kk * inv + EPSILON
        u = lax.rsqrt(v + r)
        uu = u * u * inv
        c = -uu / (1.0 + jnp.sqrt(r) * u)
        gain = uu * (o - m_k)
        masked_c = masks[b][s : s + 1] * g_c
        masked_b = mines[b][s : s + 1] * g_b
        alpha_c = masked_c * c
        alpha_b = masked_b * c
        mean = mean + masked_c * gain
        mean_own = mean_own + masked_b * gain
        h_c = g_c + alpha_c * g_kk
        h_b = g_b + alpha_b * g_kk
        alpha_ref[k : k + 1, :] = alpha_b
        anomaly_ref[k : k + 1, :] = g_a
        for i in range((k + 1) // SUBLANES, blocks):
            g_i = c_rows[i][:, k : k + 1]
            alpha_i = (turns[i][:, k : k + 1] * g_i) * c
            c_rows[i] = c_rows[i] + alpha_i * h_c + g_i * alpha_c
            b_rows[i] = b_rows[i] + alpha_i * h_b + g_i * alpha_b
            a_rows[i] = a_rows[i] + alpha_i * g_a

    transform = lax.dot_general(
        anomaly_ref[...], alpha_ref[...], (((0,), (0,)), ((), ())), precision=HIGHEST, preferred_element_type=F32
    )
    transform = transform[:members] + mean_own + (iota((members, LANES), 0) == iota((members, LANES), 1)).astype(F32)
    hi = transform[:, :members].astype(BF16)
    lo = (transform[:, :members] - hi.astype(F32)).astype(BF16)

    fetch_hi.wait()
    fetch_lo.wait()
    for p in range(planes):
        result = jnp.dot(hi, hi_ref[p], preferred_element_type=F32)
        result = result + jnp.dot(lo, hi_ref[p], preferred_element_type=F32)
        result = result + jnp.dot(hi, lo_ref[p], preferred_element_type=F32)
        for q in range(rows):
            wide_ref[p % 2, pl.ds(q, members, stride=rows), :] = result[:, q * cols : (q + 1) * cols]
        out_ref[p] = wide_ref[p % 2].astype(BF16)
        pltpu.make_async_copy(out_ref.at[p], out_hbm.at[p], out_sem.at[p]).start()
    for p in range(planes):
        pltpu.make_async_copy(out_ref.at[p], out_hbm.at[p], out_sem.at[p]).wait()


def shifted(x, axis, by, closed):
    count = lax.axis_size(axis)
    pairs = [(i, (i + by) % count) for i in range(count) if closed or 0 <= i + by < count]
    return lax.ppermute(x, axis, pairs)


def summed(x, axis):
    count = lax.axis_size(axis)
    step = 1
    while step < count:
        x = x + lax.ppermute(x, axis, [(i, i ^ step) for i in range(count)])
        step *= 2
    return x


def per_device(prior_state, courant, obs_tile, obs_site, obs_value, obs_var, loc_bits, batch_order):
    fields, levels, members, rows, cols = prior_state.shape
    planes, depth = fields * levels, members * rows
    n_lat, n_lon = lax.axis_size("lat"), lax.axis_size("lon")
    nobs = obs_tile.shape[0]
    x = prior_state.reshape(planes, depth, cols)
    winds = courant.reshape(2 * levels * rows, cols)
    tile = obs_tile.reshape(1, nobs)
    site = obs_site.reshape(1, nobs)

    payload = pl.pallas_call(
        functools.partial(observe_kernel, n_lat, n_lon, levels),
        out_shape=jax.ShapeDtypeStruct((members + members // 2 + SUBLANES, LANES), F32),
        in_specs=[VMEM, VMEM, VMEM, VMEM, SMEM],
        out_specs=VMEM,
        compiler_params=PARAMS,
        name="observe",
    )(x, winds, tile, site, batch_order)

    row_type = jax.ShapeDtypeStruct((planes, members, cols), BF16)
    column_type = jax.ShapeDtypeStruct((planes, rows, LANES), F32)
    first_row, last_row, first_col, last_col = pl.pallas_call(
        functools.partial(edges_kernel, rows),
        out_shape=[row_type, row_type, column_type, column_type],
        in_specs=[VMEM],
        out_specs=[VMEM] * 4,
        scratch_shapes=[pltpu.VMEM((depth, cols), F32)],
        compiler_params=PARAMS,
        name="edges",
    )(x)
    south = shifted(last_row, "lat", 1, False)
    north = shifted(first_row, "lat", -1, False)
    west = shifted(last_col, "lon", 1, True)
    east = shifted(first_col, "lon", -1, True)

    payload = summed(payload, "lon")
    payload = summed(payload, "lat")

    split_type = jax.ShapeDtypeStruct((planes, members, rows * cols), BF16)
    hi, lo = pl.pallas_call(
        functools.partial(forecast_kernel, levels),
        out_shape=[split_type, split_type],
        in_specs=[VMEM] * 6,
        out_specs=[VMEM] * 2,
        scratch_shapes=[pltpu.VMEM((depth, cols), F32), pltpu.VMEM((2, members, cols), F32)],
        compiler_params=PARAMS,
        name="forecast",
    )(x, winds, south, north, west, east)

    out = pl.pallas_call(
        functools.partial(analysis_kernel, n_lon, rows),
        out_shape=jax.ShapeDtypeStruct((planes, depth, cols), BF16),
        in_specs=[SMEM, SMEM, SMEM, VMEM, VMEM, VMEM, HBM, HBM],
        out_specs=HBM,
        scratch_shapes=[
            pltpu.VMEM(split_type.shape, BF16),
            pltpu.VMEM(split_type.shape, BF16),
            pltpu.VMEM((planes, depth, cols), BF16),
            pltpu.VMEM((2, depth, cols), F32),
            pltpu.VMEM((nobs, LANES), F32),
            pltpu.VMEM((nobs, LANES), F32),
            pltpu.SemaphoreType.DMA((2,)),
            pltpu.SemaphoreType.DMA((planes,)),
        ],
        compiler_params=PARAMS,
        name="analysis",
    )(batch_order, obs_value, obs_var, payload, tile, loc_bits, hi, lo)
    return out.reshape(prior_state.shape)


def solution(mesh):
    placed = (P(None, None, None, "lat", "lon"), P(None, None, "lat", "lon")) + (P(),) * 6
    return jax.shard_map(
        per_device,
        mesh=mesh,
        in_specs=placed,
        out_specs=P(None, None, None, "lat", "lon"),
        check_vma=False,
    )
```

```python
import functools

import jax
import jax.numpy as jnp
from jax import lax
from jax.experimental import pallas as pl
from jax.experimental.pallas import tpu as pltpu
from jax.sharding import PartitionSpec as P

EPSILON = 1e-05
HIGHEST = lax.Precision.HIGHEST
LANES = 128
PLAN = {"columns": 0, "pair": 2, "odd": 2, "inner": {1: [(0, 5)], 2: [(5, 8)]}, "settle": {0: ["column"], 2: ["pair_rows", "odd_rows"], 4:["pair"]}}
SUBLANES = 8
F32 = jnp.float32
BF16 = jnp.bfloat16
VMEM = pl.BlockSpec(memory_space=pltpu.VMEM)
SMEM = pl.BlockSpec(memory_space=pltpu.SMEM)
HBM = pl.BlockSpec(memory_space=pltpu.HBM)
SMALL = pl.CostEstimate(flops=0, bytes_accessed=0, transcendentals=0)
PARAMS = pltpu.CompilerParams(vmem_limit_bytes=16 * 1024 * 1024)


def iota(shape, dim):
    return lax.broadcasted_iota(jnp.int32, shape, dim)


def in_order(row, order_ref):
    nobs = row.shape[1]
    batches = order_ref.shape[0]
    batch = nobs // batches
    wide = jnp.concatenate([row, jnp.zeros((1, LANES - nobs), row.dtype)], axis=1)
    wide = jnp.broadcast_to(wide, (SUBLANES, LANES))
    lane = iota((SUBLANES, LANES), 1)
    result = jnp.zeros_like(wide)
    for i in range(batches):
        moved = pltpu.roll(wide, lax.rem(i * batch - order_ref[i] * batch + LANES, LANES), 1)
        result = jnp.where(lane // batch == i, moved, result)
    return result


def observe_kernel(
    n_lon, levels, x_hbm, courant_hbm, tile_hbm, site_hbm, order_hbm, pay_ref, x_ref, courant_ref, tile_ref, site_ref, order_ref, x_sem, sem
):
    planes, depth, cols = x_ref.shape
    small = [
        pltpu.make_async_copy(source, target, sem.at[i])
        for i, (source, target) in enumerate(
            ((order_hbm, order_ref), (tile_hbm, tile_ref), (site_hbm, site_ref), (courant_hbm, courant_ref))
        )
    ]
    for copy in small:
        copy.start()
    pieces = x_sem.shape[0]
    piece = depth // pieces
    large = [
        pltpu.make_async_copy(
            x_hbm.at[:, i * piece : (i + 1) * piece, :], x_ref.at[:, i * piece : (i + 1) * piece, :], x_sem.at[i]
        )
        for i in range(pieces)
    ]
    for copy in large:
        copy.start()
    for copy in small:
        copy.wait()
    rows = courant_ref.shape[0] // (2 * levels)
    members = depth // rows
    nobs = tile_ref.shape[1]
    cells = rows * cols
    my_lat, my_lon = lax.axis_index("lat"), lax.axis_index("lon")
    me = my_lat * n_lon + my_lon

    tile = in_order(tile_ref[...], order_ref)
    site = in_order(site_ref[...], order_ref)
    tile = tile + pltpu.roll(tile, nobs, 1)
    site = site + pltpu.roll(site, nobs, 1)
    shape = (SUBLANES, LANES)
    lane = iota(shape, 1)
    sub = iota(shape, 0)
    first = lane < nobs
    plane = site // cells
    row = (site // cols) % rows
    col = site % cols
    level = plane % levels
    lat, lon = tile // n_lon, tile % n_lon
    owner = tile == me
    from_west = (lat == my_lat) & ((lon + n_lon - 1) % n_lon == my_lon) & (col == 0)
    from_east = (lat == my_lat) & ((lon + 1) % n_lon == my_lon) & (col == cols - 1)
    from_south = (lat - 1 == my_lat) & (lon == my_lon) & (row == 0)
    from_north = (lat + 1 == my_lat) & (lon == my_lon) & (row == rows - 1)
    beside = from_west | from_east
    above = from_south | from_north
    far_col = jnp.where(from_west, cols - 1, jnp.where(from_east, 0, jnp.where(above, col, -1)))
    far_row = jnp.where(from_south, rows - 1, jnp.where(from_north, 0, row))

    down = iota((cols, LANES), 0)
    picked = jnp.dot(
        courant_ref[...], (down == col[:1]).astype(F32), precision=HIGHEST, preferred_element_type=F32
    )
    which = iota((2 * levels * rows, LANES), 0)
    at_cell = (level * rows + row)[:1]
    cu = jnp.sum(jnp.where(which == at_cell, picked, 0.0), axis=0, keepdims=True)
    cv = jnp.sum(jnp.where(which == at_cell + levels * rows, picked, 0.0), axis=0, keepdims=True)
    west, east = jnp.maximum(cu, 0.0), -jnp.minimum(cu, 0.0)
    south, north = jnp.maximum(cv, 0.0), -jnp.minimum(cv, 0.0)
    centre = 1.0 - west - east - south - north

    zero = jnp.zeros(shape, F32)
    own_rows = jnp.where(sub == row, centre, zero)
    own_rows = jnp.where(sub == row - 1, south, own_rows)
    own_rows = jnp.where(sub == row + 1, north, own_rows)
    half0 = jnp.where(first, own_rows, jnp.where(sub == row, west, zero))
    half0 = jnp.where(owner, half0, zero)
    half1 = jnp.where(first, jnp.where(owner & (sub == row), east, zero), ((beside | above) & (sub == far_row)).astype(F32))
    col0 = jnp.where(first, col, jnp.where(col > 0, col - 1, -1))
    col1 = jnp.where(first, jnp.where(col < cols - 1, col + 1, -1), far_col)
    at = jnp.concatenate([jnp.where(c < 0, -1, plane * cols + c)[:1] for c in (col0, col1)], axis=1)
    picks = (iota((planes * cols, 2 * LANES), 0) == at).astype(F32).astype(BF16)
    weights = jnp.concatenate([half0, half1], axis=1)
    for copy in large:
        copy.wait()
    block = jnp.concatenate([x_ref[p] for p in range(planes)], axis=1)
    values = jnp.dot(block, picks, preferred_element_type=F32).reshape(members, rows, 2 * LANES)
    both = jnp.sum(values * weights[None], axis=1)
    low, high = both[:, :LANES], both[:, LANES:]
    lane_m = iota((members, LANES), 1)
    own = jnp.where(lane_m < nobs, low + pltpu.roll(low, nobs, 1) + high, 0.0)
    far = jnp.where(lane_m < nobs, 0.0, high)
    put_split(pay_ref, 0, own, nobs)
    along_lon = pltpu.roll(jnp.where(beside[:1], far, 0.0), nobs, 1)
    pay_ref[members : 2 * members, :] = (along_lon + jnp.where(above[:1], far, 0.0)).astype(BF16)
    factor_lon = jnp.where(col == 0, west, jnp.where(col == cols - 1, east, zero))
    factor_lat = jnp.where(row == 0, south, jnp.where(row == rows - 1, north, zero))
    factors = jnp.where(owner, jnp.where(first, factor_lon, factor_lat), zero)
    coarse = factors.astype(BF16)
    fine = (factors - coarse.astype(F32)).astype(BF16)
    pay_ref[2 * members :, :] = jnp.concatenate([coarse, fine], axis=0)


def put_split(ref, start, values, nobs):
    coarse = values.astype(BF16)
    fine = (values - coarse.astype(F32)).astype(BF16)
    both = coarse.astype(F32) + pltpu.roll(fine.astype(F32), nobs, 1)
    ref[start : start + values.shape[0], :] = both.astype(BF16)


def edge_rows_kernel(rows, facing, x_ref, row_ref, wide_ref):
    planes, depth, cols = x_ref.shape
    members = depth // rows
    upper = lax.rem(lax.axis_index("lat"), 2) == (0 if facing else 1)
    row = jnp.where(upper, rows - 1, 0)
    for p in range(planes):
        wide_ref[p] = x_ref[p].astype(F32)
        row_ref[p] = wide_ref[p, pl.ds(row, members, stride=rows), :].astype(BF16)


def edge_columns_kernel(rows, x_ref, column_ref, wide_ref):
    planes, depth, cols = x_ref.shape
    members = depth // rows
    lane = iota((members, LANES), 1)
    total = jnp.zeros((members, LANES), F32)
    for p in range(planes):
        wide_ref[p] = x_ref[p].astype(F32)
        for r in range(rows):
            n = p * rows + r
            cell = wide_ref[p, pl.ds(r, members, stride=rows), :]
            total = jnp.where(lane // 2 == n, pltpu.roll(cell, 2 * n + 1, 1) if 2 * n + 1 < LANES else cell, total)
    total = jnp.where(lane % 2 == 0, pltpu.roll(total, LANES - 1, 1), pltpu.roll(total, 1, 1))
    column_ref[...] = total.astype(BF16)


def winds_of(courant_ref, levels, p):
    rows = courant_ref.shape[0] // (2 * levels)
    level = p % levels
    cu = courant_ref[level * rows : (level + 1) * rows, :]
    cv = courant_ref[(levels + level) * rows : (levels + level + 1) * rows, :]
    return jnp.maximum(cu, 0.0), -jnp.minimum(cu, 0.0), jnp.maximum(cv, 0.0), -jnp.minimum(cv, 0.0)


def inner_kernel(levels, start, x_ref, courant_ref, inner_ref, wide_ref, factor_ref):
    planes, rows, members, cols = inner_ref.shape
    lane = iota((rows, cols), 1)
    for i in range(planes):
        p = start + i
        wide_ref[i] = x_ref[p].astype(F32)
        west, east, south, north = winds_of(courant_ref, levels, p)
        factor_ref[i, 0] = 1.0 - west - east - south - north
        factor_ref[i, 1] = jnp.where(lane == 0, 0.0, west)
        factor_ref[i, 2] = jnp.where(lane == cols - 1, 0.0, east)
        factor_ref[i, 3] = south
        factor_ref[i, 4] = north
        for m in range(0, members, SUBLANES):
            cells = [wide_ref[i, pl.ds(m * rows + r, SUBLANES, stride=rows), :] for r in range(rows)]
            for r in range(rows):
                x = cells[r]
                value = factor_ref[i, 0, r : r + 1, :] * x
                value = value + factor_ref[i, 1, r : r + 1, :] * pltpu.roll(x, 1, 1)
                value = value + factor_ref[i, 2, r : r + 1, :] * pltpu.roll(x, cols - 1, 1)
                if r > 0:
                    value = value + factor_ref[i, 3, r : r + 1, :] * cells[r - 1]
                if r < rows - 1:
                    value = value + factor_ref[i, 4, r : r + 1, :] * cells[r + 1]
                inner_ref[i, r, m : m + SUBLANES, :] = value


def tile_mask(bits, tiles):
    words = bits.shape[1]
    word = tiles // 30
    place = tiles % 30
    chosen = jnp.zeros((bits.shape[0], LANES), jnp.int32)
    for w in range(words):
        chosen = jnp.where(word == w, bits[:, w : w + 1], chosen)
    return (jnp.right_shift(chosen, place) & 1).astype(F32)


def half_kernel(full_ref, other_ref, half_ref):
    size = half_ref.shape[0]
    upper = lax.rem(lax.axis_index("lon"), 2) == 1
    total = full_ref[...].astype(F32) + other_ref[...].astype(F32)
    half_ref[...] = jnp.where(upper, total[total.shape[0] - size :], total[:size]).astype(BF16)


def join_kernel(n_lon, stages, *refs):
    own_ref, other_ref, column_ref = refs[:3]
    column_refs, out_ref = refs[3 : 3 + stages], refs[-1]
    size, block = own_ref.shape[0], column_ref.shape[0]
    other_lon = lax.bitwise_xor(lax.axis_index("lon"), 1)
    odd = jnp.where(lax.rem(other_lon, 2) == 0, lax.rem(other_lon + n_lon - 1, n_lon), other_lon)
    far = column_refs[0][...].astype(F32)
    for i in range(1, stages):
        low = (2 << i) - 1
        far = jnp.where(jnp.bitwise_and(odd, low) == low, column_refs[i][...].astype(F32), far)
    out_ref[:size, :] = (own_ref[...].astype(F32) + other_ref[:size, :].astype(F32)).astype(BF16)
    out_ref[size : size + block, :] = column_ref[...]
    out_ref[size + block :, :] = far.astype(BF16)


def split_store(f, hi_ref, lo_ref, p, start):
    cols = f.shape[1]
    hi = f.astype(BF16)
    hi_ref[p, :, start : start + cols] = hi
    lo_ref[p, :, start : start + cols] = (f - hi.astype(F32)).astype(BF16)


def edge_factor(courant_ref, levels, p, r):
    rows, cols = courant_ref.shape[0] // (2 * levels), courant_ref.shape[1]
    west, east, _, _ = winds_of(courant_ref, levels, p)
    lane = iota((rows, cols), 1)
    return jnp.where(lane == 0, west, jnp.where(lane == cols - 1, east, 0.0))[r : r + 1]


def filter_kernel(n_lon, levels, parts, *refs):
    order_ref, value_ref, var_ref, mine_half_ref, join_ref, tile_ref, bits_ref, courant_ref = refs[:8]
    inner_refs, refs = refs[8 : 8 + len(parts)], refs[8 + len(parts) :]
    transform_ref, halo_ref, hi_ref, lo_ref, alpha_ref, anomaly_ref, mask_ref, mine_ref, row_ref = refs
    planes, members, width = hi_ref.shape
    rows = courant_ref.shape[0] // (2 * levels)
    cols = width // (rows - 2)
    nobs = tile_ref.shape[1]
    batches = order_ref.shape[0]
    batch = nobs // batches
    blocks = nobs // SUBLANES
    size = mine_half_ref.shape[0]

    my_lat, my_lon = lax.axis_index("lat"), lax.axis_index("lon")
    lon_even = lax.rem(my_lon, 2) == 0
    near = join_ref[size : size + members, :].astype(F32)
    far = join_ref[size + members :, :].astype(F32)
    halo_ref[...] = jnp.where((iota((members, LANES), 1) % 2 == 0) == lon_even, near, far)

    def complete(p, r):
        first, inner = next((a, ref) for (a, z), ref in zip(parts, inner_refs, strict=True) if a <= p < z)
        n = p * rows + r
        f = inner[p - first, r] + edge_factor(courant_ref, levels, p, r) * pltpu.roll(halo_ref[...], LANES - 1 - 2 * n, 1)
        split_store(f, hi_ref, lo_ref, p, (r - 1) * cols)

    todo = [(p, r) for p in range(planes) for r in range(1, rows - 1)]
    each = -(-len(todo) // nobs)

    me = my_lat * n_lon + my_lon
    tile = in_order(tile_ref[...], order_ref)
    bits = jnp.concatenate(
        [bits_ref[pl.ds(pl.multiple_of(order_ref[i] * batch, batch), batch), :] for i in range(batches)], axis=0
    )
    mask = tile_mask(bits, tile[:1])
    mine = tile_mask(bits, jnp.full((1, LANES), me, jnp.int32))
    mask_ref[...] = mask
    mine_ref[...] = mine
    square = jnp.concatenate([mask, jnp.zeros((LANES - nobs, LANES), F32)], axis=0)
    turned = square.T

    mine_half, other_half = mine_half_ref[...].astype(F32), join_ref[:size, :].astype(F32)
    lower = jnp.where(lon_even, mine_half, other_half)
    upper = jnp.where(lon_even, other_half, mine_half)
    payload = jnp.concatenate([lower, upper[2 * size - 2 * members - 2 * SUBLANES :]], axis=0)
    own = payload[:members]
    far = payload[members : 2 * members]
    factors = payload[2 * members :]
    both = own + far * (factors[:1] + factors[SUBLANES : SUBLANES + 1])
    prior = jnp.where(iota((members, LANES), 1) < nobs, both + pltpu.roll(both, nobs, 1), 0.0)
    mean = jnp.sum(prior, axis=0, keepdims=True) * (1.0 / members)
    spread = prior - mean
    gram = lax.dot_general(spread, spread, (((0,), (0,)), ((), ())), precision=HIGHEST, preferred_element_type=F32)
    tall = jnp.concatenate([spread, jnp.zeros((LANES - members, LANES), F32)], axis=0).T

    def cut(array):
        return [array[b * SUBLANES : (b + 1) * SUBLANES] for b in range(blocks)]

    c_rows, b_rows, a_rows = cut(gram), cut(tall), cut(tall)
    turns = cut(turned)
    mean = jnp.broadcast_to(mean, (SUBLANES, LANES))
    mean_own = jnp.zeros((1, LANES), F32)
    inv = 1.0 / (members - 1)

    def whole(array, s):
        return jnp.broadcast_to(array[s : s + 1], (SUBLANES, LANES))

    def lanes(array, k):
        return jnp.broadcast_to(array[:, k : k + 1], (SUBLANES, LANES))

    for b in range(blocks):
        base = b * SUBLANES
        at = order_ref[base // batch] * batch + base % batch
        columns = [lanes(c_rows[b], base + j) for j in range(SUBLANES)]
        allowed = [lanes(turns[b], base + j) for j in range(SUBLANES)]
        entry = {(i, j): whole(columns[j], i) for j in range(SUBLANES) for i in range(j, SUBLANES)}
        allow = {(j, q): whole(allowed[q], j) for q in range(SUBLANES) for j in range(q + 1, SUBLANES)}
        means = [lanes(mean, base + j) for j in range(SUBLANES)]
        scale, alphas, afters = [], {}, {}
        for q in range(SUBLANES):
            k = base + q
            for _ in range(each):
                if todo:
                    complete(*todo.pop(0))
            r = jnp.full((SUBLANES, LANES), var_ref[at + q], F32)
            o = jnp.full((SUBLANES, LANES), value_ref[at + q], F32)
            g = entry[q, q]
            u = lax.rsqrt(g * inv + EPSILON + r)
            uu = u * u * inv
            c = -uu / (1.0 + jnp.sqrt(r) * u)
            gain = uu * (o - means[q])
            scale.append(c)
            for j in range(q + 1, SUBLANES):
                masked = allow[j, q] * entry[j, q]
                alphas[j, q] = masked * c
                afters[j, q] = entry[j, q] + alphas[j, q] * g
                means[j] = means[j] + masked * gain
            for j in range(q + 1, SUBLANES):
                for i in range(j, SUBLANES):
                    entry[i, j] = entry[i, j] + alphas[i, q] * afters[j, q] + entry[i, q] * alphas[j, q]
            g_c, g_b, g_a = whole(c_rows[b], q), whole(b_rows[b], q), whole(a_rows[b], q)
            masked_c = jnp.broadcast_to(mask_ref[k : k + 1, :], (SUBLANES, LANES)) * g_c
            masked_b = jnp.broadcast_to(mine_ref[k : k + 1, :], (SUBLANES, LANES)) * g_b
            alpha_c, alpha_b = masked_c * c, masked_b * c
            h_c, h_b = g_c + alpha_c * g, g_b + alpha_b * g
            mean = mean + masked_c * gain
            mean_own = mean_own + (masked_b * gain)[:1]
            alpha_ref[k : k + 1, :] = alpha_b[:1]
            anomaly_ref[k : k + 1, :] = g_a[:1]
            row_ref[0, k : k + 1, :] = alpha_c[:1]
            row_ref[1, k : k + 1, :] = h_c[:1]
            row_ref[2, k : k + 1, :] = h_b[:1]
            if q < SUBLANES - 1:
                g_i = columns[q]
                alpha_i = allowed[q] * g_i * c
                c_rows[b] = c_rows[b] + alpha_i * h_c + g_i * alpha_c
                b_rows[b] = b_rows[b] + alpha_i * h_b + g_i * alpha_b
                a_rows[b] = a_rows[b] + alpha_i * g_a
                for j in range(q + 1, SUBLANES):
                    columns[j] = columns[j] + alpha_i * afters[j, q] + g_i * alphas[j, q]
        for i in range(b + 1, blocks):
            columns = [lanes(c_rows[i], base + j) for j in range(SUBLANES)]
            allowed = [lanes(turns[i], base + j) for j in range(SUBLANES)]
            for q in range(SUBLANES):
                k = base + q
                g_i = columns[q]
                alpha_i = allowed[q] * g_i * scale[q]
                c_rows[i] = c_rows[i] + alpha_i * row_ref[1, k : k + 1, :] + g_i * row_ref[0, k : k + 1, :]
                b_rows[i] = b_rows[i] + alpha_i * row_ref[2, k : k + 1, :] + g_i * alpha_ref[k : k + 1, :]
                a_rows[i] = a_rows[i] + alpha_i * anomaly_ref[k : k + 1, :]
                for j in range(q + 1, SUBLANES):
                    columns[j] = columns[j] + alpha_i * afters[j, q] + g_i * alphas[j, q]

    transform = lax.dot_general(
        anomaly_ref[...], alpha_ref[...], (((0,), (0,)), ((), ())), precision=HIGHEST, preferred_element_type=F32
    )
    transform = transform[:members] + mean_own + (iota((members, LANES), 0) == iota((members, LANES), 1)).astype(F32)
    for item in todo:
        complete(*item)
    transform_ref[...] = transform


def analysis_kernel(n_lat, levels, parts, *refs):
    transform_ref, halo_ref, hi_ref, lo_ref, courant_ref, pair_ref, odd_ref = refs[:7]
    inner_refs, refs = refs[7 : 7 + len(parts)], refs[7 + len(parts) :]
    out_hbm, edge_hi_ref, edge_lo_ref, out_ref, wide_ref, out_sem = refs
    planes, members, width = hi_ref.shape
    rows = courant_ref.shape[0] // (2 * levels)
    cols = width // (rows - 2)
    my_lat = lax.axis_index("lat")
    lat_even = lax.rem(my_lat, 2) == 0
    has_south, has_north = (my_lat > 0).astype(F32), (my_lat < n_lat - 1).astype(F32)

    transform = transform_ref[:, :members]
    hi = transform.astype(BF16)
    lo = (transform - hi.astype(F32)).astype(BF16)
    for p in range(planes):
        first, inner = next((a, ref) for (a, z), ref in zip(parts, inner_refs, strict=True) if a <= p < z)
        _, _, south, north = winds_of(courant_ref, levels, p)
        near, far = pair_ref[p].astype(F32), odd_ref[p].astype(F32)
        for r in (0, rows - 1):
            n = p * rows + r
            f = inner[p - first, r] + edge_factor(courant_ref, levels, p, r) * pltpu.roll(halo_ref[...], LANES - 1 - 2 * n, 1)
            if r == 0:
                f = f + (south[:1] * has_south) * jnp.where(lat_even, far, near)
            else:
                f = f + (north[r:] * has_north) * jnp.where(lat_even, near, far)
            split_store(f, edge_hi_ref, edge_lo_ref, p, 0 if r == 0 else cols)
    for p in range(planes):
        for h_ref, l_ref, which in ((hi_ref, lo_ref, range(1, rows - 1)), (edge_hi_ref, edge_lo_ref, (0, rows - 1))):
            result = jnp.dot(hi, h_ref[p], preferred_element_type=F32)
            result = result + jnp.dot(lo, h_ref[p], preferred_element_type=F32)
            result = result + jnp.dot(hi, l_ref[p], preferred_element_type=F32)
            for i, r in enumerate(which):
                wide_ref[p % 2, pl.ds(r, members, stride=rows), :] = result[:, i * cols : (i + 1) * cols]
        out_ref[p] = wide_ref[p % 2].astype(BF16)
        pltpu.make_async_copy(out_ref.at[p], out_hbm.at[p], out_sem.at[p]).start()
    for p in range(planes):
        pltpu.make_async_copy(out_ref.at[p], out_hbm.at[p], out_sem.at[p]).wait()


def exchanged(x, axis, step):
    return lax.ppermute(x, axis, [(i, i ^ step) for i in range(lax.axis_size(axis))])


def exchanged_odd(x, axis):
    count = lax.axis_size(axis)
    return lax.ppermute(x, axis, [pair for i in range(1, count - 1, 2) for pair in ((i, i + 1), (i + 1, i))])


def per_device(prior_state, courant, obs_tile, obs_site, obs_value, obs_var, loc_bits, batch_order):
    fields, levels, members, rows, cols = prior_state.shape
    planes, depth = fields * levels, members * rows
    n_lat, n_lon = lax.axis_size("lat"), lax.axis_size("lon")
    nobs = obs_tile.shape[0]
    x = prior_state.reshape(planes, depth, cols)
    winds = courant.reshape(2 * levels * rows, cols)
    tile = obs_tile.reshape(1, nobs)
    site = obs_site.reshape(1, nobs)

    arguments = [pltpu.with_memory_space_constraint(array, pltpu.HBM) for array in (x, winds, tile, site, batch_order)]
    payload = pl.pallas_call(
        functools.partial(observe_kernel, n_lon, levels),
        out_shape=jax.ShapeDtypeStruct((2 * members + 2 * SUBLANES, LANES), BF16),
        in_specs=[HBM] * 5,
        out_specs=VMEM,
        scratch_shapes=[
            pltpu.VMEM(x.shape, BF16),
            pltpu.VMEM(winds.shape, F32),
            pltpu.VMEM(tile.shape, jnp.int32),
            pltpu.VMEM(site.shape, jnp.int32),
            pltpu.SMEM(batch_order.shape, jnp.int32),
            pltpu.SemaphoreType.DMA((5,)),
            pltpu.SemaphoreType.DMA((4,)),
        ],
        compiler_params=PARAMS,
        name="observe",
    )(*arguments)
    payload, x = lax.optimization_barrier((payload, x))

    def local(kernel, name, out, scratch, *operands):
        return pl.pallas_call(
            kernel,
            out_shape=out,
            in_specs=[VMEM] * len(operands),
            out_specs=jax.tree.map(lambda _: VMEM, out),
            scratch_shapes=scratch,
            compiler_params=PARAMS,
            cost_estimate=SMALL,
            name=name,
        )(*operands)

    def edge_rows(x, facing):
        return local(
            functools.partial(edge_rows_kernel, rows, facing),
            "edge_rows",
            jax.ShapeDtypeStruct((planes, members, cols), BF16),
            [pltpu.VMEM((planes, depth, cols), F32)],
            x,
        )

    def inner(x, start, stop):
        return local(
            functools.partial(inner_kernel, levels, start),
            "inner",
            jax.ShapeDtypeStruct((stop - start, rows, members, cols), F32),
            [pltpu.VMEM((stop - start, depth, cols), F32), pltpu.VMEM((stop - start, 5, rows, cols), F32)],
            x,
            winds,
        )

    lat_steps = [1 << i for i in range(n_lat.bit_length() - 1)]
    lon_steps = [2 << i for i in range(n_lon.bit_length() - 2)]
    size = (payload.shape[0] // 2 + 15) // 16 * 16
    half_type = jax.ShapeDtypeStruct((size, LANES), BF16)
    done = {}
    parts, inners = [], []

    def beside(stage, x):
        if stage == PLAN["columns"]:
            done["column"] = local(
                functools.partial(edge_columns_kernel, rows),
                "edge_columns",
                jax.ShapeDtypeStruct((members, LANES), BF16),
                [pltpu.VMEM((planes, depth, cols), F32)],
                x,
            )
        if stage == PLAN["pair"]:
            done["pair_rows"] = edge_rows(x, True)
            done["pair"] = exchanged(done["pair_rows"], "lat", 1)
        if stage == PLAN["odd"]:
            done["odd_rows"] = edge_rows(x, False)
            done["odd"] = exchanged_odd(done["odd_rows"], "lat")
        for start, stop in PLAN["inner"].get(stage, ()):
            parts.append((start, stop))
            inners.append(inner(x, start, stop))

    def settle(stage, *arrays):
        held = [done.pop(name) for name in PLAN["settle"].get(stage, ())]
        names = PLAN["settle"].get(stage, ())
        arrays, new, held = lax.optimization_barrier((arrays, list(inners), held))
        inners[:] = new
        done.update(zip(names, held, strict=True))
        return arrays

    other = exchanged(payload, "lon", 1)
    beside(0, x)
    half = local(half_kernel, "half", half_type, [], payload, other)
    half, x = settle(0, half, x)
    stage = 1
    for step in lat_steps:
        other = exchanged(half, "lat", step)
        beside(stage, x)
        half = half + other
        half, x = settle(stage, half, x)
        stage += 1
    block, blocks = done["column"], []
    for step in lon_steps:
        other = exchanged(jnp.concatenate([half, block], axis=0), "lon", step)
        beside(stage, x)
        block = other[size:]
        blocks.append(block)
        if step != lon_steps[-1]:
            half = half + other[:size]
            half, block, x = settle(stage, half, block, x)
            stage += 1
    join_type = jax.ShapeDtypeStruct((size + 2 * members, LANES), BF16)
    join = local(
        functools.partial(join_kernel, n_lon, len(blocks)), "join", join_type, [], half, other, done["column"], *blocks
    )
    join, x = settle(stage, join, x)
    received = exchanged(join, "lon", 1)
    beside(stage + 1, x)

    middle_type = jax.ShapeDtypeStruct((planes, members, (rows - 2) * cols), BF16)
    square_type = jax.ShapeDtypeStruct((members, LANES), F32)
    transform, halo, hi, lo = pl.pallas_call(
        functools.partial(filter_kernel, n_lon, levels, parts),
        out_shape=[square_type, square_type, middle_type, middle_type],
        in_specs=[SMEM] * 3 + [VMEM] * (5 + len(parts)),
        out_specs=[VMEM] * 4,
        scratch_shapes=[pltpu.VMEM((nobs, LANES), F32)] * 4 + [pltpu.VMEM((3, nobs, LANES), F32)],
        compiler_params=PARAMS,
        cost_estimate=SMALL,
        name="filter",
    )(batch_order, obs_value, obs_var, join[:size], received, tile, loc_bits, winds, *inners)

    edge_type = pltpu.VMEM((planes, members, 2 * cols), BF16)
    out = pl.pallas_call(
        functools.partial(analysis_kernel, n_lat, levels, parts),
        out_shape=jax.ShapeDtypeStruct((planes, depth, cols), BF16),
        in_specs=[VMEM] * (7 + len(parts)),
        out_specs=HBM,
        scratch_shapes=[
            edge_type,
            edge_type,
            pltpu.VMEM((planes, depth, cols), BF16),
            pltpu.VMEM((2, depth, cols), F32),
            pltpu.SemaphoreType.DMA((planes,)),
        ],
        compiler_params=PARAMS,
        name="analysis",
    )(transform, halo, hi, lo, winds, done["pair"], done["odd"], *inners)
    return out.reshape(prior_state.shape)


def solution(mesh):
    placed = (P(None, None, None, "lat", "lon"), P(None, None, "lat", "lon")) + (P(),) * 6
    return jax.shard_map(
        per_device,
        mesh=mesh,
        in_specs=placed,
        out_specs=P(None, None, None, "lat", "lon"),
        check_vma=False,
    )
```

```python
import functools

import jax
import jax.numpy as jnp
from jax import lax
from jax.experimental import pallas as pl
from jax.experimental.pallas import tpu as pltpu
from jax.sharding import PartitionSpec as P

EPSILON = 1e-05
HIGHEST = lax.Precision.HIGHEST
LANES = 128
PLAN = {"filter": 0, "columns": 0, "pair": 2, "odd": 2, "inner": {1: [(0, 5)], 2: [(5, 8)]}, "settle": {0: ["column"], 2: ["pair_rows", "odd_rows"]}}
SUBLANES = 8
F32 = jnp.float32
BF16 = jnp.bfloat16
VMEM = pl.BlockSpec(memory_space=pltpu.VMEM)
SMEM = pl.BlockSpec(memory_space=pltpu.SMEM)
HBM = pl.BlockSpec(memory_space=pltpu.HBM)
SMALL = pl.CostEstimate(flops=0, bytes_accessed=0, transcendentals=0)
PARAMS = pltpu.CompilerParams(vmem_limit_bytes=16 * 1024 * 1024)


def iota(shape, dim):
    return lax.broadcasted_iota(jnp.int32, shape, dim)


def in_order(row, order_ref):
    nobs = row.shape[1]
    batches = order_ref.shape[0]
    batch = nobs // batches
    wide = jnp.concatenate([row, jnp.zeros((1, LANES - nobs), row.dtype)], axis=1)
    wide = jnp.broadcast_to(wide, (SUBLANES, LANES))
    lane = iota((SUBLANES, LANES), 1)
    result = jnp.zeros_like(wide)
    for i in range(batches):
        moved = pltpu.roll(wide, lax.rem(i * batch - order_ref[i] * batch + LANES, LANES), 1)
        result = jnp.where(lane // batch == i, moved, result)
    return result


def observe_kernel(
    n_lon, levels, x_hbm, courant_hbm, tile_hbm, site_hbm, order_hbm, pay_ref, x_ref, courant_ref, tile_ref, site_ref, order_ref, x_sem, sem
):
    planes, depth, cols = x_ref.shape
    small = [
        pltpu.make_async_copy(source, target, sem.at[i])
        for i, (source, target) in enumerate(
            ((order_hbm, order_ref), (tile_hbm, tile_ref), (site_hbm, site_ref), (courant_hbm, courant_ref))
        )
    ]
    for copy in small:
        copy.start()
    pieces = x_sem.shape[0]
    piece = depth // pieces
    large = [
        pltpu.make_async_copy(
            x_hbm.at[:, i * piece : (i + 1) * piece, :], x_ref.at[:, i * piece : (i + 1) * piece, :], x_sem.at[i]
        )
        for i in range(pieces)
    ]
    for copy in large:
        copy.start()
    for copy in small:
        copy.wait()
    rows = courant_ref.shape[0] // (2 * levels)
    members = depth // rows
    nobs = tile_ref.shape[1]
    cells = rows * cols
    my_lat, my_lon = lax.axis_index("lat"), lax.axis_index("lon")
    me = my_lat * n_lon + my_lon

    tile = in_order(tile_ref[...], order_ref)
    site = in_order(site_ref[...], order_ref)
    tile = tile + pltpu.roll(tile, nobs, 1)
    site = site + pltpu.roll(site, nobs, 1)
    shape = (SUBLANES, LANES)
    lane = iota(shape, 1)
    sub = iota(shape, 0)
    first = lane < nobs
    plane = site // cells
    row = (site // cols) % rows
    col = site % cols
    level = plane % levels
    lat, lon = tile // n_lon, tile % n_lon
    owner = tile == me
    from_west = (lat == my_lat) & ((lon + n_lon - 1) % n_lon == my_lon) & (col == 0)
    from_east = (lat == my_lat) & ((lon + 1) % n_lon == my_lon) & (col == cols - 1)
    from_south = (lat - 1 == my_lat) & (lon == my_lon) & (row == 0)
    from_north = (lat + 1 == my_lat) & (lon == my_lon) & (row == rows - 1)
    beside = from_west | from_east
    above = from_south | from_north
    far_col = jnp.where(from_west, cols - 1, jnp.where(from_east, 0, jnp.where(above, col, -1)))
    far_row = jnp.where(from_south, rows - 1, jnp.where(from_north, 0, row))

    down = iota((cols, LANES), 0)
    picked = jnp.dot(
        courant_ref[...], (down == col[:1]).astype(F32), precision=HIGHEST, preferred_element_type=F32
    )
    which = iota((2 * levels * rows, LANES), 0)
    at_cell = (level * rows + row)[:1]
    cu = jnp.sum(jnp.where(which == at_cell, picked, 0.0), axis=0, keepdims=True)
    cv = jnp.sum(jnp.where(which == at_cell + levels * rows, picked, 0.0), axis=0, keepdims=True)
    west, east = jnp.maximum(cu, 0.0), -jnp.minimum(cu, 0.0)
    south, north = jnp.maximum(cv, 0.0), -jnp.minimum(cv, 0.0)
    centre = 1.0 - west - east - south - north

    zero = jnp.zeros(shape, F32)
    own_rows = jnp.where(sub == row, centre, zero)
    own_rows = jnp.where(sub == row - 1, south, own_rows)
    own_rows = jnp.where(sub == row + 1, north, own_rows)
    half0 = jnp.where(first, own_rows, jnp.where(sub == row, west, zero))
    half0 = jnp.where(owner, half0, zero)
    half1 = jnp.where(first, jnp.where(owner & (sub == row), east, zero), ((beside | above) & (sub == far_row)).astype(F32))
    col0 = jnp.where(first, col, jnp.where(col > 0, col - 1, -1))
    col1 = jnp.where(first, jnp.where(col < cols - 1, col + 1, -1), far_col)
    at = jnp.concatenate([jnp.where(c < 0, -1, plane * cols + c)[:1] for c in (col0, col1)], axis=1)
    picks = (iota((planes * cols, 2 * LANES), 0) == at).astype(F32).astype(BF16)
    weights = jnp.concatenate([half0, half1], axis=1)
    for copy in large:
        copy.wait()
    block = jnp.concatenate([x_ref[p] for p in range(planes)], axis=1)
    values = jnp.dot(block, picks, preferred_element_type=F32).reshape(members, rows, 2 * LANES)
    both = jnp.sum(values * weights[None], axis=1)
    low, high = both[:, :LANES], both[:, LANES:]
    lane_m = iota((members, LANES), 1)
    own = jnp.where(lane_m < nobs, low + pltpu.roll(low, nobs, 1) + high, 0.0)
    far = jnp.where(lane_m < nobs, 0.0, high)
    put_split(pay_ref, 0, own, nobs)
    along_lon = pltpu.roll(jnp.where(beside[:1], far, 0.0), nobs, 1)
    pay_ref[members : 2 * members, :] = (along_lon + jnp.where(above[:1], far, 0.0)).astype(BF16)
    factor_lon = jnp.where(col == 0, west, jnp.where(col == cols - 1, east, zero))
    factor_lat = jnp.where(row == 0, south, jnp.where(row == rows - 1, north, zero))
    factors = jnp.where(owner, jnp.where(first, factor_lon, factor_lat), zero)
    coarse = factors.astype(BF16)
    fine = (factors - coarse.astype(F32)).astype(BF16)
    pay_ref[2 * members :, :] = jnp.concatenate([coarse, fine], axis=0)


def put_split(ref, start, values, nobs):
    coarse = values.astype(BF16)
    fine = (values - coarse.astype(F32)).astype(BF16)
    both = coarse.astype(F32) + pltpu.roll(fine.astype(F32), nobs, 1)
    ref[start : start + values.shape[0], :] = both.astype(BF16)


def edge_rows_kernel(rows, facing, x_ref, row_ref, wide_ref):
    planes, depth, cols = x_ref.shape
    members = depth // rows
    upper = lax.rem(lax.axis_index("lat"), 2) == (0 if facing else 1)
    row = jnp.where(upper, rows - 1, 0)
    for p in range(planes):
        wide_ref[p] = x_ref[p].astype(F32)
        row_ref[p] = wide_ref[p, pl.ds(row, members, stride=rows), :].astype(BF16)


def edge_columns_kernel(rows, x_ref, column_ref, wide_ref):
    planes, depth, cols = x_ref.shape
    members = depth // rows
    lane = iota((members, LANES), 1)
    total = jnp.zeros((members, LANES), F32)
    for p in range(planes):
        wide_ref[p] = x_ref[p].astype(F32)
        for r in range(rows):
            n = p * rows + r
            cell = wide_ref[p, pl.ds(r, members, stride=rows), :]
            total = jnp.where(lane // 2 == n, pltpu.roll(cell, 2 * n + 1, 1) if 2 * n + 1 < LANES else cell, total)
    total = jnp.where(lane % 2 == 0, pltpu.roll(total, LANES - 1, 1), pltpu.roll(total, 1, 1))
    column_ref[...] = total.astype(BF16)


def winds_of(courant_ref, levels, p):
    rows = courant_ref.shape[0] // (2 * levels)
    level = p % levels
    cu = courant_ref[level * rows : (level + 1) * rows, :]
    cv = courant_ref[(levels + level) * rows : (levels + level + 1) * rows, :]
    return jnp.maximum(cu, 0.0), -jnp.minimum(cu, 0.0), jnp.maximum(cv, 0.0), -jnp.minimum(cv, 0.0)


def inner_kernel(levels, start, x_ref, courant_ref, inner_ref, wide_ref, factor_ref):
    planes, rows, members, cols = inner_ref.shape
    lane = iota((rows, cols), 1)
    for i in range(planes):
        p = start + i
        wide_ref[i] = x_ref[p].astype(F32)
        west, east, south, north = winds_of(courant_ref, levels, p)
        factor_ref[i, 0] = 1.0 - west - east - south - north
        factor_ref[i, 1] = jnp.where(lane == 0, 0.0, west)
        factor_ref[i, 2] = jnp.where(lane == cols - 1, 0.0, east)
        factor_ref[i, 3] = south
        factor_ref[i, 4] = north
        for m in range(0, members, SUBLANES):
            cells = [wide_ref[i, pl.ds(m * rows + r, SUBLANES, stride=rows), :] for r in range(rows)]
            for r in range(rows):
                x = cells[r]
                value = factor_ref[i, 0, r : r + 1, :] * x
                value = value + factor_ref[i, 1, r : r + 1, :] * pltpu.roll(x, 1, 1)
                value = value + factor_ref[i, 2, r : r + 1, :] * pltpu.roll(x, cols - 1, 1)
                if r > 0:
                    value = value + factor_ref[i, 3, r : r + 1, :] * cells[r - 1]
                if r < rows - 1:
                    value = value + factor_ref[i, 4, r : r + 1, :] * cells[r + 1]
                inner_ref[i, r, m : m + SUBLANES, :] = value


def tile_mask(bits, tiles):
    words = bits.shape[1]
    word = tiles // 30
    place = tiles % 30
    chosen = jnp.zeros((bits.shape[0], LANES), jnp.int32)
    for w in range(words):
        chosen = jnp.where(word == w, bits[:, w : w + 1], chosen)
    return (jnp.right_shift(chosen, place) & 1).astype(F32)


def half_kernel(full_ref, other_ref, half_ref):
    size = half_ref.shape[0]
    upper = lax.rem(lax.axis_index("lon"), 2) == 1
    total = full_ref[...].astype(F32) + other_ref[...].astype(F32)
    half_ref[...] = jnp.where(upper, total[total.shape[0] - size :], total[:size]).astype(BF16)


def join_kernel(n_lon, stages, *refs):
    own_ref, other_ref, column_ref = refs[:3]
    column_refs, out_ref = refs[3 : 3 + stages], refs[-1]
    size, block = own_ref.shape[0], column_ref.shape[0]
    other_lon = lax.bitwise_xor(lax.axis_index("lon"), 1)
    odd = jnp.where(lax.rem(other_lon, 2) == 0, lax.rem(other_lon + n_lon - 1, n_lon), other_lon)
    far = column_refs[0][...].astype(F32)
    for i in range(1, stages):
        low = (2 << i) - 1
        far = jnp.where(jnp.bitwise_and(odd, low) == low, column_refs[i][...].astype(F32), far)
    out_ref[:size, :] = (own_ref[...].astype(F32) + other_ref[:size, :].astype(F32)).astype(BF16)
    out_ref[size : size + block, :] = column_ref[...]
    out_ref[size + block :, :] = far.astype(BF16)


def split_store(f, hi_ref, lo_ref, p, start):
    cols = f.shape[1]
    hi = f.astype(BF16)
    hi_ref[p, :, start : start + cols] = hi
    lo_ref[p, :, start : start + cols] = (f - hi.astype(F32)).astype(BF16)


def edge_factor(courant_ref, levels, p, r):
    rows, cols = courant_ref.shape[0] // (2 * levels), courant_ref.shape[1]
    west, east, _, _ = winds_of(courant_ref, levels, p)
    lane = iota((rows, cols), 1)
    return jnp.where(lane == 0, west, jnp.where(lane == cols - 1, east, 0.0))[r : r + 1]


def filter_kernel(n_lon, levels, parts, *refs):
    order_ref, value_ref, var_ref, mine_half_ref, join_ref, tile_ref, bits_ref, courant_ref = refs[:8]
    inner_refs, refs = refs[8 : 8 + len(parts)], refs[8 + len(parts) :]
    transform_ref, halo_ref, hi_ref, lo_ref, alpha_ref, anomaly_ref, mask_ref, mine_ref, row_ref, move_ref = refs
    planes, members, width = hi_ref.shape
    rows = courant_ref.shape[0] // (2 * levels)
    cols = width // (rows - 2)
    nobs = tile_ref.shape[1]
    batches = order_ref.shape[0]
    batch = nobs // batches
    blocks = nobs // SUBLANES
    size = mine_half_ref.shape[0]

    my_lat, my_lon = lax.axis_index("lat"), lax.axis_index("lon")
    lon_even = lax.rem(my_lon, 2) == 0
    near = join_ref[size : size + members, :].astype(F32)
    far = join_ref[size + members :, :].astype(F32)
    halo_ref[...] = jnp.where((iota((members, LANES), 1) % 2 == 0) == lon_even, near, far)

    def complete(p, r):
        first, inner = next((a, ref) for (a, z), ref in zip(parts, inner_refs, strict=True) if a <= p < z)
        n = p * rows + r
        f = inner[p - first, r] + edge_factor(courant_ref, levels, p, r) * pltpu.roll(halo_ref[...], LANES - 1 - 2 * n, 1)
        split_store(f, hi_ref, lo_ref, p, (r - 1) * cols)

    todo = [(p, r) for p in range(planes) for r in range(1, rows - 1)]
    each = -(-len(todo) // nobs)

    me = my_lat * n_lon + my_lon
    tile = in_order(tile_ref[...], order_ref)
    bits = jnp.concatenate(
        [bits_ref[pl.ds(pl.multiple_of(order_ref[i] * batch, batch), batch), :] for i in range(batches)], axis=0
    )
    mask = tile_mask(bits, tile[:1])
    mine = tile_mask(bits, jnp.full((1, LANES), me, jnp.int32))
    mask_ref[...] = mask
    mine_ref[...] = mine
    square = jnp.concatenate([mask, jnp.zeros((LANES - nobs, LANES), F32)], axis=0)
    turned = square.T

    mine_half, other_half = mine_half_ref[...].astype(F32), join_ref[:size, :].astype(F32)
    lower = jnp.where(lon_even, mine_half, other_half)
    upper = jnp.where(lon_even, other_half, mine_half)
    payload = jnp.concatenate([lower, upper[2 * size - 2 * members - 2 * SUBLANES :]], axis=0)
    own = payload[:members]
    far = payload[members : 2 * members]
    factors = payload[2 * members :]
    both = own + far * (factors[:1] + factors[SUBLANES : SUBLANES + 1])
    prior = jnp.where(iota((members, LANES), 1) < nobs, both + pltpu.roll(both, nobs, 1), 0.0)
    mean = jnp.sum(prior, axis=0, keepdims=True) * (1.0 / members)
    spread = prior - mean
    inv = 1.0 / (members - 1)
    gram = inv * lax.dot_general(spread, spread, (((0,), (0,)), ((), ())), precision=HIGHEST, preferred_element_type=F32)
    tall = jnp.concatenate([spread, jnp.zeros((LANES - members, LANES), F32)], axis=0).T

    def cut(array):
        return [array[b * SUBLANES : (b + 1) * SUBLANES] for b in range(blocks)]

    c_rows, b_rows, a_rows = cut(gram), cut(tall * inv), cut(tall)
    turns = cut(turned)
    mean = jnp.broadcast_to(mean, (SUBLANES, LANES))
    mean_own = jnp.zeros((1, LANES), F32)

    def whole(array, s):
        return jnp.broadcast_to(array[s : s + 1], (SUBLANES, LANES))

    def lanes(array, k):
        return jnp.broadcast_to(array[:, k : k + 1], (SUBLANES, LANES))

    for b in range(blocks):
        base = b * SUBLANES
        at = order_ref[base // batch] * batch + base % batch
        ahead = range(b, min(b + 3, blocks))
        columns = {i: [lanes(c_rows[i], base + j) for j in range(SUBLANES)] for i in ahead}
        allowed = {i: [lanes(turns[i], base + j) for j in range(SUBLANES)] for i in ahead}
        place = move_ref.at[b % 2]
        for j in range(SUBLANES):
            place[4 + j] = columns[b][j]
            place[12 + j] = allowed[b][j]

        def taken(i, s):
            return jnp.broadcast_to(move_ref[b % 2, i, s : s + 1, :], (SUBLANES, LANES))

        entry = {(i, j): taken(4 + j, i) for j in range(SUBLANES) for i in range(j, SUBLANES)}
        allow = {(j, q): taken(12 + q, j) for q in range(SUBLANES) for j in range(q + 1, SUBLANES)}
        means = [lanes(mean, base + j) for j in range(SUBLANES)]
        alphas, afters = {}, {}
        for q in range(SUBLANES):
            k = base + q
            for _ in range(each):
                if todo:
                    complete(*todo.pop(0))
            r = jnp.full((SUBLANES, LANES), var_ref[at + q], F32)
            o = jnp.full((SUBLANES, LANES), value_ref[at + q], F32)
            g = entry[q, q]
            u = lax.rsqrt(total if q else g + (r + EPSILON))
            uu = u * u
            c = -uu * pl.reciprocal(1.0 + jnp.sqrt(r) * u, approx=True)
            gain = uu * (o - means[q])
            if q + 1 < SUBLANES:
                g_j, masked = entry[q + 1, q], allow[q + 1, q] * entry[q + 1, q]
                next_r = jnp.full((SUBLANES, LANES), var_ref[at + q + 1], F32) + EPSILON
                total = (entry[q + 1, q + 1] + next_r) + c * (2.0 * masked * g_j + c * (masked * masked * g))
            for j in range(q + 1, SUBLANES):
                masked = allow[j, q] * entry[j, q]
                alphas[j, q] = masked * c
                afters[j, q] = entry[j, q] + alphas[j, q] * g
                means[j] = means[j] + masked * gain
            for j in range(q + 1, SUBLANES):
                for i in range(j, SUBLANES):
                    entry[i, j] = entry[i, j] + alphas[i, q] * afters[j, q] + entry[i, q] * alphas[j, q]
            g_c, g_b, g_a = whole(c_rows[b], q), whole(b_rows[b], q), whole(a_rows[b], q)
            masked_c = jnp.broadcast_to(mask_ref[k : k + 1, :], (SUBLANES, LANES)) * g_c
            masked_b = jnp.broadcast_to(mine_ref[k : k + 1, :], (SUBLANES, LANES)) * g_b
            alpha_c, alpha_b = masked_c * c, masked_b * c
            h_c, h_b = g_c + alpha_c * g, g_b + alpha_b * g
            mean = mean + masked_c * gain
            mean_own = mean_own + (masked_b * gain)[:1]
            alpha_ref[k : k + 1, :] = alpha_b[:1]
            anomaly_ref[k : k + 1, :] = g_a[:1]
            row_ref[0, k : k + 1, :] = alpha_c[:1]
            row_ref[1, k : k + 1, :] = h_c[:1]
            row_ref[2, k : k + 1, :] = h_b[:1]
            row_ref[3, k : k + 1, :] = g_c[:1]
            for i in ahead:
                if i == b and q == SUBLANES - 1:
                    continue
                g_i = columns[i][q]
                alpha_i = allowed[i][q] * g_i * c
                c_rows[i] = c_rows[i] + alpha_i * h_c + g_i * alpha_c
                b_rows[i] = b_rows[i] + alpha_i * h_b + g_i * alpha_b
                a_rows[i] = a_rows[i] + alpha_i * g_a
                for j in range(q + 1, SUBLANES):
                    columns[i][j] = columns[i][j] + alpha_i * afters[j, q] + g_i * alphas[j, q]
        if b + 3 < blocks:
            own = slice(base, base + SUBLANES)
            alpha_c, h_c, h_b, g_c = (row_ref[i, own, :] for i in range(4))
            left = jnp.concatenate([alpha_c, g_c], axis=0)[:, :nobs]
            zero = jnp.zeros((SUBLANES, LANES), F32)
            upper = jnp.concatenate([h_c, h_b, anomaly_ref[own, :]], axis=1)
            right = jnp.concatenate([upper, jnp.concatenate([alpha_c, alpha_ref[own, :], zero], axis=1)], axis=0)
            change = lax.dot_general(left, right, (((0,), (0,)), ((), ())), precision=HIGHEST, preferred_element_type=F32)
            for i in range(b + 3, blocks):
                part = change[i * SUBLANES : (i + 1) * SUBLANES]
                c_rows[i] = c_rows[i] + part[:, :LANES]
                b_rows[i] = b_rows[i] + part[:, LANES : 2 * LANES]
                a_rows[i] = a_rows[i] + part[:, 2 * LANES :]

    transform = lax.dot_general(
        anomaly_ref[...], alpha_ref[...], (((0,), (0,)), ((), ())), precision=HIGHEST, preferred_element_type=F32
    )
    transform = transform[:members] + mean_own + (iota((members, LANES), 0) == iota((members, LANES), 1)).astype(F32)
    for item in todo:
        complete(*item)
    transform_ref[...] = transform


def analysis_kernel(n_lat, levels, parts, *refs):
    transform_ref, halo_ref, hi_ref, lo_ref, courant_ref, pair_ref, odd_ref = refs[:7]
    inner_refs, refs = refs[7 : 7 + len(parts)], refs[7 + len(parts) :]
    out_hbm, edge_hi_ref, edge_lo_ref, out_ref, wide_ref, out_sem = refs
    planes, members, width = hi_ref.shape
    rows = courant_ref.shape[0] // (2 * levels)
    cols = width // (rows - 2)
    my_lat = lax.axis_index("lat")
    lat_even = lax.rem(my_lat, 2) == 0
    has_south, has_north = (my_lat > 0).astype(F32), (my_lat < n_lat - 1).astype(F32)

    transform = transform_ref[:, :members]
    hi = transform.astype(BF16)
    lo = (transform - hi.astype(F32)).astype(BF16)
    for p in range(planes):
        first, inner = next((a, ref) for (a, z), ref in zip(parts, inner_refs, strict=True) if a <= p < z)
        _, _, south, north = winds_of(courant_ref, levels, p)
        near, far = pair_ref[p].astype(F32), odd_ref[p].astype(F32)
        for r in (0, rows - 1):
            n = p * rows + r
            f = inner[p - first, r] + edge_factor(courant_ref, levels, p, r) * pltpu.roll(halo_ref[...], LANES - 1 - 2 * n, 1)
            if r == 0:
                f = f + (south[:1] * has_south) * jnp.where(lat_even, far, near)
            else:
                f = f + (north[r:] * has_north) * jnp.where(lat_even, near, far)
            split_store(f, edge_hi_ref, edge_lo_ref, p, 0 if r == 0 else cols)
    for p in range(planes):
        for h_ref, l_ref, which in ((hi_ref, lo_ref, range(1, rows - 1)), (edge_hi_ref, edge_lo_ref, (0, rows - 1))):
            result = jnp.dot(hi, h_ref[p], preferred_element_type=F32)
            result = result + jnp.dot(lo, h_ref[p], preferred_element_type=F32)
            result = result + jnp.dot(hi, l_ref[p], preferred_element_type=F32)
            for i, r in enumerate(which):
                wide_ref[p % 2, pl.ds(r, members, stride=rows), :] = result[:, i * cols : (i + 1) * cols]
        out_ref[p] = wide_ref[p % 2].astype(BF16)
        pltpu.make_async_copy(out_ref.at[p], out_hbm.at[p], out_sem.at[p]).start()
    for p in range(planes):
        pltpu.make_async_copy(out_ref.at[p], out_hbm.at[p], out_sem.at[p]).wait()


def exchanged(x, axis, step):
    return lax.ppermute(x, axis, [(i, i ^ step) for i in range(lax.axis_size(axis))])


def exchanged_odd(x, axis):
    count = lax.axis_size(axis)
    return lax.ppermute(x, axis, [pair for i in range(1, count, 2) for pair in ((i, (i + 1) % count), ((i + 1) % count, i))])


def per_device(prior_state, courant, obs_tile, obs_site, obs_value, obs_var, loc_bits, batch_order):
    fields, levels, members, rows, cols = prior_state.shape
    planes, depth = fields * levels, members * rows
    n_lat, n_lon = lax.axis_size("lat"), lax.axis_size("lon")
    nobs = obs_tile.shape[0]
    x = prior_state.reshape(planes, depth, cols)
    winds = courant.reshape(2 * levels * rows, cols)
    tile = obs_tile.reshape(1, nobs)
    site = obs_site.reshape(1, nobs)

    arguments = [pltpu.with_memory_space_constraint(array, pltpu.HBM) for array in (x, winds, tile, site, batch_order)]
    payload = pl.pallas_call(
        functools.partial(observe_kernel, n_lon, levels),
        out_shape=jax.ShapeDtypeStruct((2 * members + 2 * SUBLANES, LANES), BF16),
        in_specs=[HBM] * 5,
        out_specs=VMEM,
        scratch_shapes=[
            pltpu.VMEM(x.shape, BF16),
            pltpu.VMEM(winds.shape, F32),
            pltpu.VMEM(tile.shape, jnp.int32),
            pltpu.VMEM(site.shape, jnp.int32),
            pltpu.SMEM(batch_order.shape, jnp.int32),
            pltpu.SemaphoreType.DMA((5,)),
            pltpu.SemaphoreType.DMA((4,)),
        ],
        compiler_params=PARAMS,
        name="observe",
    )(*arguments)
    payload, x = lax.optimization_barrier((payload, x))

    def local(kernel, name, out, scratch, *operands):
        return pl.pallas_call(
            kernel,
            out_shape=out,
            in_specs=[VMEM] * len(operands),
            out_specs=jax.tree.map(lambda _: VMEM, out),
            scratch_shapes=scratch,
            compiler_params=PARAMS,
            cost_estimate=SMALL,
            name=name,
        )(*operands)

    def edge_rows(x, facing):
        return local(
            functools.partial(edge_rows_kernel, rows, facing),
            "edge_rows",
            jax.ShapeDtypeStruct((planes, members, cols), BF16),
            [pltpu.VMEM((planes, depth, cols), F32)],
            x,
        )

    def inner(x, start, stop):
        return local(
            functools.partial(inner_kernel, levels, start),
            "inner",
            jax.ShapeDtypeStruct((stop - start, rows, members, cols), F32),
            [pltpu.VMEM((stop - start, depth, cols), F32), pltpu.VMEM((stop - start, 5, rows, cols), F32)],
            x,
            winds,
        )

    lat_steps = [1 << i for i in range(n_lat.bit_length() - 1)]
    lon_steps = [2 << i for i in range(n_lon.bit_length() - 2)]
    size = (payload.shape[0] // 2 + 15) // 16 * 16
    half_type = jax.ShapeDtypeStruct((size, LANES), BF16)
    done = {}
    parts, inners = [], []

    def beside(stage, x):
        if stage == PLAN["columns"]:
            done["column"] = local(
                functools.partial(edge_columns_kernel, rows),
                "edge_columns",
                jax.ShapeDtypeStruct((members, LANES), BF16),
                [pltpu.VMEM((planes, depth, cols), F32)],
                x,
            )
        if stage == PLAN["pair"]:
            done["pair_rows"] = edge_rows(x, True)
            done["pair"] = exchanged(done["pair_rows"], "lat", 1)
        if stage == PLAN["odd"]:
            done["odd_rows"] = edge_rows(x, False)
            done["odd"] = exchanged_odd(done["odd_rows"], "lat")
        for start, stop in PLAN["inner"].get(stage, ()):
            parts.append((start, stop))
            inners.append(inner(x, start, stop))

    def settle(stage, *arrays):
        held = [done.pop(name) for name in PLAN["settle"].get(stage, ())]
        names = PLAN["settle"].get(stage, ())
        arrays, new, held = lax.optimization_barrier((arrays, list(inners), held))
        inners[:] = new
        done.update(zip(names, held, strict=True))
        return arrays

    other = exchanged(payload, "lon", 1)
    beside(0, x)
    half = local(half_kernel, "half", half_type, [], payload, other)
    half, x = settle(0, half, x)
    stage = 1
    for step in lat_steps:
        other = exchanged(half, "lat", step)
        beside(stage, x)
        half = half + other
        half, x = settle(stage, half, x)
        stage += 1
    block, blocks = done["column"], []
    for step in lon_steps:
        other = exchanged(jnp.concatenate([half, block], axis=0), "lon", step)
        beside(stage, x)
        block = other[size:]
        blocks.append(block)
        if step != lon_steps[-1]:
            half = half + other[:size]
            half, block, x = settle(stage, half, block, x)
            stage += 1
    join_type = jax.ShapeDtypeStruct((size + 2 * members, LANES), BF16)
    join = local(
        functools.partial(join_kernel, n_lon, len(blocks)), "join", join_type, [], half, other, done["column"], *blocks
    )
    join, x = settle(stage, join, x)
    received = exchanged(join, "lon", 1)
    beside(stage + 1, x)

    middle_type = jax.ShapeDtypeStruct((planes, members, (rows - 2) * cols), BF16)
    square_type = jax.ShapeDtypeStruct((members, LANES), F32)
    transform, halo, hi, lo = pl.pallas_call(
        functools.partial(filter_kernel, n_lon, levels, parts),
        out_shape=[square_type, square_type, middle_type, middle_type],
        in_specs=[SMEM] * 3 + [VMEM] * (5 + len(parts)),
        out_specs=[VMEM] * 4,
        scratch_shapes=[pltpu.VMEM((nobs, LANES), F32)] * 4 + [pltpu.VMEM((4, nobs, LANES), F32), pltpu.VMEM((2, 32, SUBLANES, LANES), F32)],
        compiler_params=PARAMS,
        cost_estimate=pl.CostEstimate(flops=0, bytes_accessed=PLAN["filter"], transcendentals=0),
        name="filter",
    )(batch_order, obs_value, obs_var, join[:size], received, tile, loc_bits, winds, *inners)

    edge_type = pltpu.VMEM((planes, members, 2 * cols), BF16)
    out = pl.pallas_call(
        functools.partial(analysis_kernel, n_lat, levels, parts),
        out_shape=jax.ShapeDtypeStruct((planes, depth, cols), BF16),
        in_specs=[VMEM] * (7 + len(parts)),
        out_specs=HBM,
        scratch_shapes=[
            edge_type,
            edge_type,
            pltpu.VMEM((planes, depth, cols), BF16),
            pltpu.VMEM((2, depth, cols), F32),
            pltpu.SemaphoreType.DMA((planes,)),
        ],
        compiler_params=PARAMS,
        name="analysis",
    )(transform, halo, hi, lo, winds, done["pair"], done["odd"], *inners)
    return out.reshape(prior_state.shape)


def solution(mesh):
    placed = (P(None, None, None, "lat", "lon"), P(None, None, "lat", "lon")) + (P(),) * 6
    return jax.shard_map(
        per_device,
        mesh=mesh,
        in_specs=placed,
        out_specs=P(None, None, None, "lat", "lon"),
        check_vma=False,
    )
```

```python
import functools

import jax
import jax.numpy as jnp
from jax import lax
from jax.experimental import pallas as pl
from jax.experimental.pallas import tpu as pltpu
from jax.sharding import PartitionSpec as P

EPSILON = 1e-05
HIGHEST = lax.Precision.HIGHEST
LANES = 128
PLAN = {"filter": 0, "columns": 0, "pair": 2, "odd": 2, "inner": {1: [(0, 5)], 2: [(5, 8)]}, "settle": {0: ["column"], 2: ["pair_rows", "odd_rows"]}}
SUBLANES = 8
F32 = jnp.float32
BF16 = jnp.bfloat16
VMEM = pl.BlockSpec(memory_space=pltpu.VMEM)
SMEM = pl.BlockSpec(memory_space=pltpu.SMEM)
HBM = pl.BlockSpec(memory_space=pltpu.HBM)
SMALL = pl.CostEstimate(flops=0, bytes_accessed=0, transcendentals=0)
PARAMS = pltpu.CompilerParams(vmem_limit_bytes=16 * 1024 * 1024)


def iota(shape, dim):
    return lax.broadcasted_iota(jnp.int32, shape, dim)


def in_order(row, order_ref):
    nobs = row.shape[1]
    batches = order_ref.shape[0]
    batch = nobs // batches
    wide = jnp.concatenate([row, jnp.zeros((1, LANES - nobs), row.dtype)], axis=1)
    wide = jnp.broadcast_to(wide, (SUBLANES, LANES))
    lane = iota((SUBLANES, LANES), 1)
    result = jnp.zeros_like(wide)
    for i in range(batches):
        moved = pltpu.roll(wide, lax.rem(i * batch - order_ref[i] * batch + LANES, LANES), 1)
        result = jnp.where(lane // batch == i, moved, result)
    return result


def observe_kernel(
    n_lon, levels, x_hbm, courant_hbm, tile_hbm, site_hbm, order_hbm, pay_ref, x_ref, courant_ref, tile_ref, site_ref, order_ref, x_sem, sem
):
    planes, depth, cols = x_ref.shape
    small = [
        pltpu.make_async_copy(source, target, sem.at[i])
        for i, (source, target) in enumerate(
            ((order_hbm, order_ref), (tile_hbm, tile_ref), (site_hbm, site_ref), (courant_hbm, courant_ref))
        )
    ]
    for copy in small:
        copy.start()
    pieces = x_sem.shape[0]
    share = planes // pieces
    large = [
        pltpu.make_async_copy(x_hbm.at[i * share : (i + 1) * share], x_ref.at[i * share : (i + 1) * share], x_sem.at[i])
        for i in range(pieces)
    ]
    for copy in large:
        copy.start()
    for copy in small:
        copy.wait()
    rows = courant_ref.shape[0] // (2 * levels)
    members = depth // rows
    nobs = tile_ref.shape[1]
    cells = rows * cols
    my_lat, my_lon = lax.axis_index("lat"), lax.axis_index("lon")
    me = my_lat * n_lon + my_lon

    tile = in_order(tile_ref[...], order_ref)
    site = in_order(site_ref[...], order_ref)
    tile = tile + pltpu.roll(tile, nobs, 1)
    site = site + pltpu.roll(site, nobs, 1)
    shape = (SUBLANES, LANES)
    lane = iota(shape, 1)
    sub = iota(shape, 0)
    first = lane < nobs
    plane = site // cells
    row = (site // cols) % rows
    col = site % cols
    level = plane % levels
    lat, lon = tile // n_lon, tile % n_lon
    owner = tile == me
    from_west = (lat == my_lat) & ((lon + n_lon - 1) % n_lon == my_lon) & (col == 0)
    from_east = (lat == my_lat) & ((lon + 1) % n_lon == my_lon) & (col == cols - 1)
    from_south = (lat - 1 == my_lat) & (lon == my_lon) & (row == 0)
    from_north = (lat + 1 == my_lat) & (lon == my_lon) & (row == rows - 1)
    beside = from_west | from_east
    above = from_south | from_north
    far_col = jnp.where(from_west, cols - 1, jnp.where(from_east, 0, jnp.where(above, col, -1)))
    far_row = jnp.where(from_south, rows - 1, jnp.where(from_north, 0, row))

    down = iota((cols, LANES), 0)
    picked = jnp.dot(
        courant_ref[...], (down == col[:1]).astype(F32), precision=HIGHEST, preferred_element_type=F32
    )
    which = iota((2 * levels * rows, LANES), 0)
    at_cell = (level * rows + row)[:1]
    cu = jnp.sum(jnp.where(which == at_cell, picked, 0.0), axis=0, keepdims=True)
    cv = jnp.sum(jnp.where(which == at_cell + levels * rows, picked, 0.0), axis=0, keepdims=True)
    west, east = jnp.maximum(cu, 0.0), -jnp.minimum(cu, 0.0)
    south, north = jnp.maximum(cv, 0.0), -jnp.minimum(cv, 0.0)
    centre = 1.0 - west - east - south - north

    zero = jnp.zeros(shape, F32)
    own_rows = jnp.where(sub == row, centre, zero)
    own_rows = jnp.where(sub == row - 1, south, own_rows)
    own_rows = jnp.where(sub == row + 1, north, own_rows)
    half0 = jnp.where(first, own_rows, jnp.where(sub == row, west, zero))
    half0 = jnp.where(owner, half0, zero)
    half1 = jnp.where(first, jnp.where(owner & (sub == row), east, zero), ((beside | above) & (sub == far_row)).astype(F32))
    col0 = jnp.where(first, col, jnp.where(col > 0, col - 1, -1))
    col1 = jnp.where(first, jnp.where(col < cols - 1, col + 1, -1), far_col)
    at = jnp.concatenate([jnp.where(c < 0, -1, plane * cols + c)[:1] for c in (col0, col1)], axis=1)
    picks = (iota((planes * cols, 2 * LANES), 0) == at).astype(F32).astype(BF16)
    weights = jnp.concatenate([half0, half1], axis=1)
    values = None
    for i in range(pieces):
        large[i].wait()
        block = jnp.concatenate([x_ref[p] for p in range(i * share, (i + 1) * share)], axis=1)
        part = jnp.dot(block, picks[i * share * cols : (i + 1) * share * cols], preferred_element_type=F32)
        values = part if values is None else values + part
    values = values.reshape(members, rows, 2 * LANES)
    both = jnp.sum(values * weights[None], axis=1)
    low, high = both[:, :LANES], both[:, LANES:]
    lane_m = iota((members, LANES), 1)
    own = jnp.where(lane_m < nobs, low + pltpu.roll(low, nobs, 1) + high, 0.0)
    far = jnp.where(lane_m < nobs, 0.0, high)
    put_split(pay_ref, 0, own, nobs)
    along_lon = pltpu.roll(jnp.where(beside[:1], far, 0.0), nobs, 1)
    pay_ref[members : 2 * members, :] = (along_lon + jnp.where(above[:1], far, 0.0)).astype(BF16)
    factor_lon = jnp.where(col == 0, west, jnp.where(col == cols - 1, east, zero))
    factor_lat = jnp.where(row == 0, south, jnp.where(row == rows - 1, north, zero))
    factors = jnp.where(owner, jnp.where(first, factor_lon, factor_lat), zero)
    coarse = factors.astype(BF16)
    fine = (factors - coarse.astype(F32)).astype(BF16)
    pay_ref[2 * members :, :] = jnp.concatenate([coarse, fine], axis=0)


def put_split(ref, start, values, nobs):
    coarse = values.astype(BF16)
    fine = (values - coarse.astype(F32)).astype(BF16)
    both = coarse.astype(F32) + pltpu.roll(fine.astype(F32), nobs, 1)
    ref[start : start + values.shape[0], :] = both.astype(BF16)


def edge_rows_kernel(rows, facing, x_ref, row_ref, wide_ref):
    planes, depth, cols = x_ref.shape
    members = depth // rows
    upper = lax.rem(lax.axis_index("lat"), 2) == (0 if facing else 1)
    row = jnp.where(upper, rows - 1, 0)
    for p in range(planes):
        wide_ref[p] = x_ref[p].astype(F32)
        row_ref[p] = wide_ref[p, pl.ds(row, members, stride=rows), :].astype(BF16)


def edge_columns_kernel(rows, x_ref, column_ref, wide_ref):
    planes, depth, cols = x_ref.shape
    members = depth // rows
    lane = iota((members, LANES), 1)
    total = jnp.zeros((members, LANES), F32)
    for p in range(planes):
        wide_ref[p] = x_ref[p].astype(F32)
        for r in range(rows):
            n = p * rows + r
            cell = wide_ref[p, pl.ds(r, members, stride=rows), :]
            total = jnp.where(lane // 2 == n, pltpu.roll(cell, 2 * n + 1, 1) if 2 * n + 1 < LANES else cell, total)
    total = jnp.where(lane % 2 == 0, pltpu.roll(total, LANES - 1, 1), pltpu.roll(total, 1, 1))
    column_ref[...] = total.astype(BF16)


def winds_of(courant_ref, levels, p):
    rows = courant_ref.shape[0] // (2 * levels)
    level = p % levels
    cu = courant_ref[level * rows : (level + 1) * rows, :]
    cv = courant_ref[(levels + level) * rows : (levels + level + 1) * rows, :]
    return jnp.maximum(cu, 0.0), -jnp.minimum(cu, 0.0), jnp.maximum(cv, 0.0), -jnp.minimum(cv, 0.0)


def inner_kernel(levels, start, x_ref, courant_ref, inner_ref, wide_ref, factor_ref):
    planes, rows, members, cols = inner_ref.shape
    lane = iota((rows, cols), 1)
    for i in range(planes):
        p = start + i
        wide_ref[i] = x_ref[p].astype(F32)
        west, east, south, north = winds_of(courant_ref, levels, p)
        factor_ref[i, 0] = 1.0 - west - east - south - north
        factor_ref[i, 1] = jnp.where(lane == 0, 0.0, west)
        factor_ref[i, 2] = jnp.where(lane == cols - 1, 0.0, east)
        factor_ref[i, 3] = south
        factor_ref[i, 4] = north
        for m in range(0, members, SUBLANES):
            cells = [wide_ref[i, pl.ds(m * rows + r, SUBLANES, stride=rows), :] for r in range(rows)]
            for r in range(rows):
                x = cells[r]
                value = factor_ref[i, 0, r : r + 1, :] * x
                value = value + factor_ref[i, 1, r : r + 1, :] * pltpu.roll(x, 1, 1)
                value = value + factor_ref[i, 2, r : r + 1, :] * pltpu.roll(x, cols - 1, 1)
                if r > 0:
                    value = value + factor_ref[i, 3, r : r + 1, :] * cells[r - 1]
                if r < rows - 1:
                    value = value + factor_ref[i, 4, r : r + 1, :] * cells[r + 1]
                inner_ref[i, r, m : m + SUBLANES, :] = value


def tile_mask(bits, tiles):
    words = bits.shape[1]
    word = tiles // 30
    place = tiles % 30
    chosen = jnp.zeros((bits.shape[0], LANES), jnp.int32)
    for w in range(words):
        chosen = jnp.where(word == w, bits[:, w : w + 1], chosen)
    return (jnp.right_shift(chosen, place) & 1).astype(F32)


def half_kernel(full_ref, other_ref, half_ref):
    size = half_ref.shape[0]
    upper = lax.rem(lax.axis_index("lon"), 2) == 1
    total = full_ref[...].astype(F32) + other_ref[...].astype(F32)
    half_ref[...] = jnp.where(upper, total[total.shape[0] - size :], total[:size]).astype(BF16)


def join_kernel(n_lon, stages, *refs):
    own_ref, other_ref, column_ref = refs[:3]
    column_refs, out_ref = refs[3 : 3 + stages], refs[-1]
    size, block = own_ref.shape[0], column_ref.shape[0]
    other_lon = lax.bitwise_xor(lax.axis_index("lon"), 1)
    odd = jnp.where(lax.rem(other_lon, 2) == 0, lax.rem(other_lon + n_lon - 1, n_lon), other_lon)
    far = column_refs[0][...].astype(F32)
    for i in range(1, stages):
        low = (2 << i) - 1
        far = jnp.where(jnp.bitwise_and(odd, low) == low, column_refs[i][...].astype(F32), far)
    out_ref[:size, :] = (own_ref[...].astype(F32) + other_ref[:size, :].astype(F32)).astype(BF16)
    out_ref[size : size + block, :] = column_ref[...]
    out_ref[size + block :, :] = far.astype(BF16)


def split_store(f, hi_ref, lo_ref, p, start):
    cols = f.shape[1]
    hi = f.astype(BF16)
    hi_ref[p, :, start : start + cols] = hi
    lo_ref[p, :, start : start + cols] = (f - hi.astype(F32)).astype(BF16)


def edge_factor(courant_ref, levels, p, r):
    rows, cols = courant_ref.shape[0] // (2 * levels), courant_ref.shape[1]
    west, east, _, _ = winds_of(courant_ref, levels, p)
    lane = iota((rows, cols), 1)
    return jnp.where(lane == 0, west, jnp.where(lane == cols - 1, east, 0.0))[r : r + 1]


def filter_kernel(n_lon, levels, parts, *refs):
    order_ref, value_ref, var_ref, mine_half_ref, join_ref, tile_ref, bits_ref, courant_ref = refs[:8]
    inner_refs, refs = refs[8 : 8 + len(parts)], refs[8 + len(parts) :]
    transform_ref, halo_ref, hi_ref, lo_ref, alpha_ref, anomaly_ref, mask_ref, mine_ref, row_ref, move_ref = refs
    planes, members, width = hi_ref.shape
    rows = courant_ref.shape[0] // (2 * levels)
    cols = width // (rows - 2)
    nobs = tile_ref.shape[1]
    batches = order_ref.shape[0]
    batch = nobs // batches
    blocks = nobs // SUBLANES
    size = mine_half_ref.shape[0]

    my_lat, my_lon = lax.axis_index("lat"), lax.axis_index("lon")
    lon_even = lax.rem(my_lon, 2) == 0
    near = join_ref[size : size + members, :].astype(F32)
    far = join_ref[size + members :, :].astype(F32)
    halo_ref[...] = jnp.where((iota((members, LANES), 1) % 2 == 0) == lon_even, near, far)

    def complete(p, r):
        first, inner = next((a, ref) for (a, z), ref in zip(parts, inner_refs, strict=True) if a <= p < z)
        n = p * rows + r
        f = inner[p - first, r] + edge_factor(courant_ref, levels, p, r) * pltpu.roll(halo_ref[...], LANES - 1 - 2 * n, 1)
        split_store(f, hi_ref, lo_ref, p, (r - 1) * cols)

    todo = [(p, r) for p in range(planes) for r in range(1, rows - 1)]
    each = -(-len(todo) // nobs)

    me = my_lat * n_lon + my_lon
    tile = in_order(tile_ref[...], order_ref)
    bits = jnp.concatenate(
        [bits_ref[pl.ds(pl.multiple_of(order_ref[i] * batch, batch), batch), :] for i in range(batches)], axis=0
    )
    mask = tile_mask(bits, tile[:1])
    mine = tile_mask(bits, jnp.full((1, LANES), me, jnp.int32))
    mask_ref[...] = mask
    mine_ref[...] = mine
    square = jnp.concatenate([mask, jnp.zeros((LANES - nobs, LANES), F32)], axis=0)
    turned = square.T

    mine_half, other_half = mine_half_ref[...].astype(F32), join_ref[:size, :].astype(F32)
    lower = jnp.where(lon_even, mine_half, other_half)
    upper = jnp.where(lon_even, other_half, mine_half)
    payload = jnp.concatenate([lower, upper[2 * size - 2 * members - 2 * SUBLANES :]], axis=0)
    own = payload[:members]
    far = payload[members : 2 * members]
    factors = payload[2 * members :]
    both = own + far * (factors[:1] + factors[SUBLANES : SUBLANES + 1])
    prior = jnp.where(iota((members, LANES), 1) < nobs, both + pltpu.roll(both, nobs, 1), 0.0)
    mean = jnp.sum(prior, axis=0, keepdims=True) * (1.0 / members)
    spread = prior - mean
    inv = 1.0 / (members - 1)
    gram = inv * lax.dot_general(spread, spread, (((0,), (0,)), ((), ())), precision=HIGHEST, preferred_element_type=F32)
    tall = jnp.concatenate([spread, jnp.zeros((LANES - members, LANES), F32)], axis=0).T

    def cut(array):
        return [array[b * SUBLANES : (b + 1) * SUBLANES] for b in range(blocks)]

    c_rows, b_rows, a_rows = cut(gram), cut(tall * inv), cut(tall)
    turns = cut(turned)
    mean = jnp.broadcast_to(mean, (SUBLANES, LANES))
    mean_own = jnp.zeros((1, LANES), F32)

    def whole(array, s):
        return jnp.broadcast_to(array[s : s + 1], (SUBLANES, LANES))

    def lanes(array, k):
        return jnp.broadcast_to(array[:, k : k + 1], (SUBLANES, LANES))

    for b in range(blocks):
        base = b * SUBLANES
        at = order_ref[base // batch] * batch + base % batch
        ahead = range(b, min(b + 3, blocks))
        columns = {i: [lanes(c_rows[i], base + j) for j in range(SUBLANES)] for i in ahead}
        allowed = {i: [lanes(turns[i], base + j) for j in range(SUBLANES)] for i in ahead}
        place = move_ref.at[b % 2]
        for j in range(SUBLANES):
            place[4 + j] = columns[b][j]
            place[12 + j] = allowed[b][j]

        def taken(i, s):
            return jnp.broadcast_to(move_ref[b % 2, i, s : s + 1, :], (SUBLANES, LANES))

        entry = {(i, j): taken(4 + j, i) for j in range(SUBLANES) for i in range(j, SUBLANES)}
        allow = {(j, q): taken(12 + q, j) for q in range(SUBLANES) for j in range(q + 1, SUBLANES)}
        means = [lanes(mean, base + j) for j in range(SUBLANES)]
        alphas, afters = {}, {}
        for q in range(SUBLANES):
            k = base + q
            for _ in range(each):
                if todo:
                    complete(*todo.pop(0))
            r = jnp.full((SUBLANES, LANES), var_ref[at + q], F32)
            o = jnp.full((SUBLANES, LANES), value_ref[at + q], F32)
            g = entry[q, q]
            u = lax.rsqrt(total if q else g + (r + EPSILON))
            uu = u * u
            c = -uu * pl.reciprocal(1.0 + jnp.sqrt(r) * u, approx=True)
            gain = uu * (o - means[q])
            if q + 1 < SUBLANES:
                g_j, masked = entry[q + 1, q], allow[q + 1, q] * entry[q + 1, q]
                next_r = jnp.full((SUBLANES, LANES), var_ref[at + q + 1], F32) + EPSILON
                total = (entry[q + 1, q + 1] + next_r) + c * (2.0 * masked * g_j + c * (masked * masked * g))
            for j in range(q + 1, SUBLANES):
                masked = allow[j, q] * entry[j, q]
                alphas[j, q] = masked * c
                afters[j, q] = entry[j, q] + alphas[j, q] * g
                means[j] = means[j] + masked * gain
            for j in range(q + 1, SUBLANES):
                for i in range(j, SUBLANES):
                    entry[i, j] = entry[i, j] + alphas[i, q] * afters[j, q] + entry[i, q] * alphas[j, q]
            g_c, g_b, g_a = whole(c_rows[b], q), whole(b_rows[b], q), whole(a_rows[b], q)
            masked_c = jnp.broadcast_to(mask_ref[k : k + 1, :], (SUBLANES, LANES)) * g_c
            masked_b = jnp.broadcast_to(mine_ref[k : k + 1, :], (SUBLANES, LANES)) * g_b
            alpha_c, alpha_b = masked_c * c, masked_b * c
            h_c, h_b = g_c + alpha_c * g, g_b + alpha_b * g
            mean = mean + masked_c * gain
            mean_own = mean_own + (masked_b * gain)[:1]
            alpha_ref[k : k + 1, :] = alpha_b[:1]
            anomaly_ref[k : k + 1, :] = g_a[:1]
            row_ref[0, k : k + 1, :] = alpha_c[:1]
            row_ref[1, k : k + 1, :] = h_c[:1]
            row_ref[2, k : k + 1, :] = h_b[:1]
            row_ref[3, k : k + 1, :] = g_c[:1]
            for i in ahead:
                if i == b and q == SUBLANES - 1:
                    continue
                g_i = columns[i][q]
                alpha_i = allowed[i][q] * g_i * c
                c_rows[i] = c_rows[i] + alpha_i * h_c + g_i * alpha_c
                b_rows[i] = b_rows[i] + alpha_i * h_b + g_i * alpha_b
                a_rows[i] = a_rows[i] + alpha_i * g_a
                for j in range(q + 1, SUBLANES):
                    columns[i][j] = columns[i][j] + alpha_i * afters[j, q] + g_i * alphas[j, q]
        if b + 3 < blocks:
            own = slice(base, base + SUBLANES)
            alpha_c, h_c, h_b, g_c = (row_ref[i, own, :] for i in range(4))
            left = jnp.concatenate([alpha_c, g_c], axis=0)[:, :nobs]
            zero = jnp.zeros((SUBLANES, LANES), F32)
            upper = jnp.concatenate([h_c, h_b, anomaly_ref[own, :]], axis=1)
            right = jnp.concatenate([upper, jnp.concatenate([alpha_c, alpha_ref[own, :], zero], axis=1)], axis=0)
            change = lax.dot_general(left, right, (((0,), (0,)), ((), ())), precision=HIGHEST, preferred_element_type=F32)
            for i in range(b + 3, blocks):
                part = change[i * SUBLANES : (i + 1) * SUBLANES]
                c_rows[i] = c_rows[i] + part[:, :LANES]
                b_rows[i] = b_rows[i] + part[:, LANES : 2 * LANES]
                a_rows[i] = a_rows[i] + part[:, 2 * LANES :]

    transform = lax.dot_general(
        anomaly_ref[...], alpha_ref[...], (((0,), (0,)), ((), ())), precision=HIGHEST, preferred_element_type=F32
    )
    transform = transform[:members] + mean_own + (iota((members, LANES), 0) == iota((members, LANES), 1)).astype(F32)
    for item in todo:
        complete(*item)
    transform_ref[...] = transform


def analysis_kernel(n_lat, levels, parts, *refs):
    transform_ref, halo_ref, hi_ref, lo_ref, courant_ref, pair_ref, odd_ref = refs[:7]
    inner_refs, refs = refs[7 : 7 + len(parts)], refs[7 + len(parts) :]
    out_hbm, edge_hi_ref, edge_lo_ref, out_ref, wide_ref, out_sem = refs
    planes, members, width = hi_ref.shape
    rows = courant_ref.shape[0] // (2 * levels)
    cols = width // (rows - 2)
    my_lat = lax.axis_index("lat")
    lat_even = lax.rem(my_lat, 2) == 0
    has_south, has_north = (my_lat > 0).astype(F32), (my_lat < n_lat - 1).astype(F32)

    transform = transform_ref[...]
    hi = transform.astype(BF16).astype(F32)
    lo = transform - hi
    lane = iota((members, LANES), 1)
    spill = 2 * members - LANES
    left = jnp.where(lane < members, hi, pltpu.roll(lo, members, 1))
    right = jnp.where(lane < spill, pltpu.roll(lo, members, 1), pltpu.roll(hi, spill, 1))
    terms = jnp.concatenate([left, right], axis=1).astype(BF16)[:, : 3 * members]
    for p in range(planes):
        first, inner = next((a, ref) for (a, z), ref in zip(parts, inner_refs, strict=True) if a <= p < z)
        _, _, south, north = winds_of(courant_ref, levels, p)
        near, far = pair_ref[p].astype(F32), odd_ref[p].astype(F32)
        for r in (0, rows - 1):
            n = p * rows + r
            f = inner[p - first, r] + edge_factor(courant_ref, levels, p, r) * pltpu.roll(halo_ref[...], LANES - 1 - 2 * n, 1)
            if r == 0:
                f = f + (south[:1] * has_south) * jnp.where(lat_even, far, near)
            else:
                f = f + (north[r:] * has_north) * jnp.where(lat_even, near, far)
            split_store(f, edge_hi_ref, edge_lo_ref, p, 0 if r == 0 else cols)
    for p in range(planes):
        for h_ref, l_ref, which in ((hi_ref, lo_ref, range(1, rows - 1)), (edge_hi_ref, edge_lo_ref, (0, rows - 1))):
            stacked = jnp.concatenate([h_ref[p], h_ref[p], l_ref[p]], axis=0)
            result = jnp.dot(terms, stacked, preferred_element_type=F32)
            for i, r in enumerate(which):
                wide_ref[p % 2, pl.ds(r, members, stride=rows), :] = result[:, i * cols : (i + 1) * cols]
        out_ref[p] = wide_ref[p % 2].astype(BF16)
        pltpu.make_async_copy(out_ref.at[p], out_hbm.at[p], out_sem.at[p]).start()
    for p in range(planes):
        pltpu.make_async_copy(out_ref.at[p], out_hbm.at[p], out_sem.at[p]).wait()


def exchanged(x, axis, step):
    return lax.ppermute(x, axis, [(i, i ^ step) for i in range(lax.axis_size(axis))])


def exchanged_odd(x, axis):
    count = lax.axis_size(axis)
    return lax.ppermute(x, axis, [pair for i in range(1, count, 2) for pair in ((i, (i + 1) % count), ((i + 1) % count, i))])


def per_device(prior_state, courant, obs_tile, obs_site, obs_value, obs_var, loc_bits, batch_order):
    fields, levels, members, rows, cols = prior_state.shape
    planes, depth = fields * levels, members * rows
    n_lat, n_lon = lax.axis_size("lat"), lax.axis_size("lon")
    nobs = obs_tile.shape[0]
    x = prior_state.reshape(planes, depth, cols)
    winds = courant.reshape(2 * levels * rows, cols)
    tile = obs_tile.reshape(1, nobs)
    site = obs_site.reshape(1, nobs)

    arguments = [pltpu.with_memory_space_constraint(array, pltpu.HBM) for array in (x, winds, tile, site, batch_order)]
    payload = pl.pallas_call(
        functools.partial(observe_kernel, n_lon, levels),
        out_shape=jax.ShapeDtypeStruct((2 * members + 2 * SUBLANES, LANES), BF16),
        in_specs=[HBM] * 5,
        out_specs=VMEM,
        scratch_shapes=[
            pltpu.VMEM(x.shape, BF16),
            pltpu.VMEM(winds.shape, F32),
            pltpu.VMEM(tile.shape, jnp.int32),
            pltpu.VMEM(site.shape, jnp.int32),
            pltpu.SMEM(batch_order.shape, jnp.int32),
            pltpu.SemaphoreType.DMA((1,)),
            pltpu.SemaphoreType.DMA((4,)),
        ],
        compiler_params=PARAMS,
        name="observe",
    )(*arguments)
    payload, x = lax.optimization_barrier((payload, x))

    def local(kernel, name, out, scratch, *operands):
        return pl.pallas_call(
            kernel,
            out_shape=out,
            in_specs=[VMEM] * len(operands),
            out_specs=jax.tree.map(lambda _: VMEM, out),
            scratch_shapes=scratch,
            compiler_params=PARAMS,
            cost_estimate=SMALL,
            name=name,
        )(*operands)

    def edge_rows(x, facing):
        return local(
            functools.partial(edge_rows_kernel, rows, facing),
            "edge_rows",
            jax.ShapeDtypeStruct((planes, members, cols), BF16),
            [pltpu.VMEM((planes, depth, cols), F32)],
            x,
        )

    def inner(x, start, stop):
        return local(
            functools.partial(inner_kernel, levels, start),
            "inner",
            jax.ShapeDtypeStruct((stop - start, rows, members, cols), F32),
            [pltpu.VMEM((stop - start, depth, cols), F32), pltpu.VMEM((stop - start, 5, rows, cols), F32)],
            x,
            winds,
        )

    lat_steps = [1 << i for i in range(n_lat.bit_length() - 1)]
    lon_steps = [2 << i for i in range(n_lon.bit_length() - 2)]
    size = (payload.shape[0] // 2 + 15) // 16 * 16
    half_type = jax.ShapeDtypeStruct((size, LANES), BF16)
    done = {}
    parts, inners = [], []

    def beside(stage, x):
        if stage == PLAN["columns"]:
            done["column"] = local(
                functools.partial(edge_columns_kernel, rows),
                "edge_columns",
                jax.ShapeDtypeStruct((members, LANES), BF16),
                [pltpu.VMEM((planes, depth, cols), F32)],
                x,
            )
        if stage == PLAN["pair"]:
            done["pair_rows"] = edge_rows(x, True)
            done["pair"] = exchanged(done["pair_rows"], "lat", 1)
        if stage == PLAN["odd"]:
            done["odd_rows"] = edge_rows(x, False)
            done["odd"] = exchanged_odd(done["odd_rows"], "lat")
        for start, stop in PLAN["inner"].get(stage, ()):
            parts.append((start, stop))
            inners.append(inner(x, start, stop))

    def settle(stage, *arrays):
        held = [done.pop(name) for name in PLAN["settle"].get(stage, ())]
        names = PLAN["settle"].get(stage, ())
        arrays, new, held = lax.optimization_barrier((arrays, list(inners), held))
        inners[:] = new
        done.update(zip(names, held, strict=True))
        return arrays

    other = exchanged(payload, "lon", 1)
    beside(0, x)
    half = local(half_kernel, "half", half_type, [], payload, other)
    half, x = settle(0, half, x)
    stage = 1
    for step in lat_steps:
        other = exchanged(half, "lat", step)
        beside(stage, x)
        half = half + other
        half, x = settle(stage, half, x)
        stage += 1
    block, blocks = done["column"], []
    for step in lon_steps:
        other = exchanged(jnp.concatenate([half, block], axis=0), "lon", step)
        beside(stage, x)
        block = other[size:]
        blocks.append(block)
        if step != lon_steps[-1]:
            half = half + other[:size]
            half, block, x = settle(stage, half, block, x)
            stage += 1
    join_type = jax.ShapeDtypeStruct((size + 2 * members, LANES), BF16)
    join = local(
        functools.partial(join_kernel, n_lon, len(blocks)), "join", join_type, [], half, other, done["column"], *blocks
    )
    join, x = settle(stage, join, x)
    received = exchanged(join, "lon", 1)
    beside(stage + 1, x)

    middle_type = jax.ShapeDtypeStruct((planes, members, (rows - 2) * cols), BF16)
    square_type = jax.ShapeDtypeStruct((members, LANES), F32)
    transform, halo, hi, lo = pl.pallas_call(
        functools.partial(filter_kernel, n_lon, levels, parts),
        out_shape=[square_type, square_type, middle_type, middle_type],
        in_specs=[SMEM] * 3 + [VMEM] * (5 + len(parts)),
        out_specs=[VMEM] * 4,
        scratch_shapes=[pltpu.VMEM((nobs, LANES), F32)] * 4 + [pltpu.VMEM((4, nobs, LANES), F32), pltpu.VMEM((2, 32, SUBLANES, LANES), F32)],
        compiler_params=PARAMS,
        cost_estimate=pl.CostEstimate(flops=0, bytes_accessed=PLAN["filter"], transcendentals=0),
        name="filter",
    )(batch_order, obs_value, obs_var, join[:size], received, tile, loc_bits, winds, *inners)

    edge_type = pltpu.VMEM((planes, members, 2 * cols), BF16)
    out = pl.pallas_call(
        functools.partial(analysis_kernel, n_lat, levels, parts),
        out_shape=jax.ShapeDtypeStruct((planes, depth, cols), BF16),
        in_specs=[VMEM] * (7 + len(parts)),
        out_specs=HBM,
        scratch_shapes=[
            edge_type,
            edge_type,
            pltpu.VMEM((planes, depth, cols), BF16),
            pltpu.VMEM((2, depth, cols), F32),
            pltpu.SemaphoreType.DMA((planes,)),
        ],
        compiler_params=PARAMS,
        name="analysis",
    )(transform, halo, hi, lo, winds, done["pair"], done["odd"], *inners)
    return out.reshape(prior_state.shape)


def solution(mesh):
    placed = (P(None, None, None, "lat", "lon"), P(None, None, "lat", "lon")) + (P(),) * 6
    return jax.shard_map(
        per_device,
        mesh=mesh,
        in_specs=placed,
        out_specs=P(None, None, None, "lat", "lon"),
        check_vma=False,
    )
```

```python
import functools

import jax
import jax.numpy as jnp
from jax import lax
from jax.experimental import pallas as pl
from jax.experimental.pallas import tpu as pltpu
from jax.sharding import PartitionSpec as P

EPSILON = 1e-05
HIGHEST = lax.Precision.HIGHEST
LANES = 128
PLAN = {"filter": 1000000000, "columns": 0, "pieces": (1, 1), "pair": 2, "pair_send": 2, "odd": 2, "odd_send": 4, "inner": {1: [(0, 5)], 2: [(5, 8)]}, "settle": {0: ["column"], 2: ["pair_rows", "odd_rows"], 3: ["odd_rows"], 4: ["pair"]}}
SUBLANES = 8
F32 = jnp.float32
BF16 = jnp.bfloat16
VMEM = pl.BlockSpec(memory_space=pltpu.VMEM)
SMEM = pl.BlockSpec(memory_space=pltpu.SMEM)
HBM = pl.BlockSpec(memory_space=pltpu.HBM)
SMALL = pl.CostEstimate(flops=0, bytes_accessed=0, transcendentals=0)
PARAMS = pltpu.CompilerParams(vmem_limit_bytes=16 * 1024 * 1024)


def iota(shape, dim):
    return lax.broadcasted_iota(jnp.int32, shape, dim)


def in_order(row, order_ref):
    nobs = row.shape[1]
    batches = order_ref.shape[0]
    batch = nobs // batches
    wide = jnp.concatenate([row, jnp.zeros((1, LANES - nobs), row.dtype)], axis=1)
    wide = jnp.broadcast_to(wide, (SUBLANES, LANES))
    lane = iota((SUBLANES, LANES), 1)
    result = jnp.zeros_like(wide)
    for i in range(batches):
        moved = pltpu.roll(wide, lax.rem(i * batch - order_ref[i] * batch + LANES, LANES), 1)
        result = jnp.where(lane // batch == i, moved, result)
    return result


def observe_kernel(
    n_lon, levels, x_hbm, courant_hbm, tile_hbm, site_hbm, order_hbm, pay_ref, x_ref, courant_ref, tile_ref, site_ref, order_ref, x_sem, sem
):
    planes, depth, cols = x_ref.shape
    small = [
        pltpu.make_async_copy(source, target, sem.at[i])
        for i, (source, target) in enumerate(
            ((order_hbm, order_ref), (tile_hbm, tile_ref), (site_hbm, site_ref), (courant_hbm, courant_ref))
        )
    ]
    for copy in small:
        copy.start()
    pieces = x_sem.shape[0]
    share = planes // pieces
    large = [
        pltpu.make_async_copy(x_hbm.at[i * share : (i + 1) * share], x_ref.at[i * share : (i + 1) * share], x_sem.at[i])
        for i in range(pieces)
    ]
    for copy in large:
        copy.start()
    for copy in small:
        copy.wait()
    rows = courant_ref.shape[0] // (2 * levels)
    members = depth // rows
    nobs = tile_ref.shape[1]
    cells = rows * cols
    my_lat, my_lon = lax.axis_index("lat"), lax.axis_index("lon")
    me = my_lat * n_lon + my_lon

    tile = in_order(tile_ref[...], order_ref)
    site = in_order(site_ref[...], order_ref)
    tile = tile + pltpu.roll(tile, nobs, 1)
    site = site + pltpu.roll(site, nobs, 1)
    shape = (SUBLANES, LANES)
    lane = iota(shape, 1)
    sub = iota(shape, 0)
    first = lane < nobs
    plane = site // cells
    row = (site // cols) % rows
    col = site % cols
    level = plane % levels
    lat, lon = tile // n_lon, tile % n_lon
    owner = tile == me
    from_west = (lat == my_lat) & ((lon + n_lon - 1) % n_lon == my_lon) & (col == 0)
    from_east = (lat == my_lat) & ((lon + 1) % n_lon == my_lon) & (col == cols - 1)
    from_south = (lat - 1 == my_lat) & (lon == my_lon) & (row == 0)
    from_north = (lat + 1 == my_lat) & (lon == my_lon) & (row == rows - 1)
    beside = from_west | from_east
    above = from_south | from_north
    far_col = jnp.where(from_west, cols - 1, jnp.where(from_east, 0, jnp.where(above, col, -1)))
    far_row = jnp.where(from_south, rows - 1, jnp.where(from_north, 0, row))

    down = iota((cols, LANES), 0)
    picked = jnp.dot(
        courant_ref[...], (down == col[:1]).astype(F32), precision=HIGHEST, preferred_element_type=F32
    )
    which = iota((2 * levels * rows, LANES), 0)
    at_cell = (level * rows + row)[:1]
    cu = jnp.sum(jnp.where(which == at_cell, picked, 0.0), axis=0, keepdims=True)
    cv = jnp.sum(jnp.where(which == at_cell + levels * rows, picked, 0.0), axis=0, keepdims=True)
    west, east = jnp.maximum(cu, 0.0), -jnp.minimum(cu, 0.0)
    south, north = jnp.maximum(cv, 0.0), -jnp.minimum(cv, 0.0)
    centre = 1.0 - west - east - south - north

    zero = jnp.zeros(shape, F32)
    own_rows = jnp.where(sub == row, centre, zero)
    own_rows = jnp.where(sub == row - 1, south, own_rows)
    own_rows = jnp.where(sub == row + 1, north, own_rows)
    half0 = jnp.where(first, own_rows, jnp.where(sub == row, west, zero))
    half0 = jnp.where(owner, half0, zero)
    half1 = jnp.where(first, jnp.where(owner & (sub == row), east, zero), ((beside | above) & (sub == far_row)).astype(F32))
    col0 = jnp.where(first, col, jnp.where(col > 0, col - 1, -1))
    col1 = jnp.where(first, jnp.where(col < cols - 1, col + 1, -1), far_col)
    at = jnp.concatenate([jnp.where(c < 0, -1, plane * cols + c)[:1] for c in (col0, col1)], axis=1)
    picks = (iota((planes * cols, 2 * LANES), 0) == at).astype(F32).astype(BF16)
    weights = jnp.concatenate([half0, half1], axis=1)
    values = None
    for i in range(pieces):
        large[i].wait()
        block = jnp.concatenate([x_ref[p] for p in range(i * share, (i + 1) * share)], axis=1)
        part = jnp.dot(block, picks[i * share * cols : (i + 1) * share * cols], preferred_element_type=F32)
        values = part if values is None else values + part
    values = values.reshape(members, rows, 2 * LANES)
    both = jnp.sum(values * weights[None], axis=1)
    low, high = both[:, :LANES], both[:, LANES:]
    lane_m = iota((members, LANES), 1)
    own = jnp.where(lane_m < nobs, low + pltpu.roll(low, nobs, 1) + high, 0.0)
    far = jnp.where(lane_m < nobs, 0.0, high)
    put_split(pay_ref, 0, own, nobs)
    along_lon = pltpu.roll(jnp.where(beside[:1], far, 0.0), nobs, 1)
    pay_ref[members : 2 * members, :] = (along_lon + jnp.where(above[:1], far, 0.0)).astype(BF16)
    factor_lon = jnp.where(col == 0, west, jnp.where(col == cols - 1, east, zero))
    factor_lat = jnp.where(row == 0, south, jnp.where(row == rows - 1, north, zero))
    factors = jnp.where(owner, jnp.where(first, factor_lon, factor_lat), zero)
    coarse = factors.astype(BF16)
    fine = (factors - coarse.astype(F32)).astype(BF16)
    pay_ref[2 * members :, :] = jnp.concatenate([coarse, fine], axis=0)


def put_split(ref, start, values, nobs):
    coarse = values.astype(BF16)
    fine = (values - coarse.astype(F32)).astype(BF16)
    both = coarse.astype(F32) + pltpu.roll(fine.astype(F32), nobs, 1)
    ref[start : start + values.shape[0], :] = both.astype(BF16)


def edge_rows_kernel(rows, facing, x_ref, *refs):
    planes, depth, cols = x_ref.shape
    members = depth // rows
    upper = lax.rem(lax.axis_index("lat"), 2) == (0 if facing else 1)
    row = jnp.where(upper, rows - 1, 0)
    *row_refs, wide_ref = refs
    share = planes // len(row_refs)
    for p in range(planes):
        wide_ref[p] = x_ref[p].astype(F32)
        row_refs[p // share][p % share] = wide_ref[p, pl.ds(row, members, stride=rows), :].astype(BF16)


def folded(values, size):
    half = values.shape[0] // 2
    odd = iota((half, LANES), 1) % 2 == 1
    both = jnp.where(odd, values[:half], pltpu.roll(values[half:], LANES - 1, 1))
    return jnp.concatenate([both, jnp.zeros((size - half, LANES), F32)], axis=0)


def unfolded(values):
    return jnp.concatenate([values, pltpu.roll(values, 1, 1)], axis=0)


def edge_columns_kernel(rows, x_ref, near_ref, far_ref, wide_ref):
    planes, depth, cols = x_ref.shape
    members = depth // rows
    lane = iota((members, LANES), 1)
    total = jnp.zeros((members, LANES), F32)
    for p in range(planes):
        wide_ref[p] = x_ref[p].astype(F32)
        for r in range(rows):
            n = p * rows + r
            cell = wide_ref[p, pl.ds(r, members, stride=rows), :]
            total = jnp.where(lane // 2 == n, pltpu.roll(cell, 2 * n + 1, 1) if 2 * n + 1 < LANES else cell, total)
    last = pltpu.roll(total, 1, 1)
    even = lax.rem(lax.axis_index("lon"), 2) == 0
    size = near_ref.shape[0]
    near_ref[...] = folded(jnp.where(even, last, total), size).astype(BF16)
    far_ref[...] = folded(jnp.where(even, total, last), size).astype(BF16)


def winds_of(courant_ref, levels, p):
    rows = courant_ref.shape[0] // (2 * levels)
    level = p % levels
    cu = courant_ref[level * rows : (level + 1) * rows, :]
    cv = courant_ref[(levels + level) * rows : (levels + level + 1) * rows, :]
    return jnp.maximum(cu, 0.0), -jnp.minimum(cu, 0.0), jnp.maximum(cv, 0.0), -jnp.minimum(cv, 0.0)


def inner_kernel(levels, start, x_ref, courant_ref, inner_ref, wide_ref, factor_ref):
    planes, rows, members, cols = inner_ref.shape
    lane = iota((rows, cols), 1)
    for i in range(planes):
        p = start + i
        wide_ref[i] = x_ref[p].astype(F32)
        west, east, south, north = winds_of(courant_ref, levels, p)
        factor_ref[i, 0] = 1.0 - west - east - south - north
        factor_ref[i, 1] = jnp.where(lane == 0, 0.0, west)
        factor_ref[i, 2] = jnp.where(lane == cols - 1, 0.0, east)
        factor_ref[i, 3] = south
        factor_ref[i, 4] = north
        for m in range(0, members, SUBLANES):
            cells = [wide_ref[i, pl.ds(m * rows + r, SUBLANES, stride=rows), :] for r in range(rows)]
            for r in range(rows):
                x = cells[r]
                value = factor_ref[i, 0, r : r + 1, :] * x
                value = value + factor_ref[i, 1, r : r + 1, :] * pltpu.roll(x, 1, 1)
                value = value + factor_ref[i, 2, r : r + 1, :] * pltpu.roll(x, cols - 1, 1)
                if r > 0:
                    value = value + factor_ref[i, 3, r : r + 1, :] * cells[r - 1]
                if r < rows - 1:
                    value = value + factor_ref[i, 4, r : r + 1, :] * cells[r + 1]
                inner_ref[i, r, m : m + SUBLANES, :] = value


def tile_mask(bits, tiles):
    words = bits.shape[1]
    word = tiles // 30
    place = tiles % 30
    chosen = jnp.zeros((bits.shape[0], LANES), jnp.int32)
    for w in range(words):
        chosen = jnp.where(word == w, bits[:, w : w + 1], chosen)
    return (jnp.right_shift(chosen, place) & 1).astype(F32)


def half_kernel(full_ref, other_ref, half_ref):
    size = half_ref.shape[0]
    upper = lax.rem(lax.axis_index("lon"), 2) == 1
    total = full_ref[...].astype(F32) + other_ref[...].astype(F32)
    half_ref[...] = jnp.where(upper, total[total.shape[0] - size :], total[:size]).astype(BF16)


def join_kernel(n_lon, stages, *refs):
    own_ref, other_ref, column_ref = refs[:3]
    column_refs, out_ref = refs[3 : 3 + stages], refs[-1]
    size, block = own_ref.shape[0], column_ref.shape[0]
    other_lon = lax.bitwise_xor(lax.axis_index("lon"), 1)
    odd = jnp.where(lax.rem(other_lon, 2) == 0, lax.rem(other_lon + n_lon - 1, n_lon), other_lon)
    far = column_refs[0][...].astype(F32)
    for i in range(1, stages):
        low = (2 << i) - 1
        far = jnp.where(jnp.bitwise_and(odd, low) == low, column_refs[i][...].astype(F32), far)
    out_ref[:size, :] = (own_ref[...].astype(F32) + other_ref[:size, :].astype(F32)).astype(BF16)
    out_ref[size : size + block, :] = column_ref[...]
    out_ref[size + block :, :] = far.astype(BF16)


def split_store(f, hi_ref, lo_ref, p, start):
    cols = f.shape[1]
    hi = f.astype(BF16)
    hi_ref[p, :, start : start + cols] = hi
    lo_ref[p, :, start : start + cols] = (f - hi.astype(F32)).astype(BF16)


def edge_factor(courant_ref, levels, p, r):
    rows, cols = courant_ref.shape[0] // (2 * levels), courant_ref.shape[1]
    west, east, _, _ = winds_of(courant_ref, levels, p)
    lane = iota((rows, cols), 1)
    return jnp.where(lane == 0, west, jnp.where(lane == cols - 1, east, 0.0))[r : r + 1]


def filter_kernel(n_lon, levels, parts, *refs):
    order_ref, value_ref, var_ref, mine_half_ref, join_ref, tile_ref, bits_ref, courant_ref = refs[:8]
    inner_refs, refs = refs[8 : 8 + len(parts)], refs[8 + len(parts) :]
    transform_ref, halo_ref, hi_ref, lo_ref, alpha_ref, anomaly_ref, mask_ref, mine_ref, row_ref, move_ref = refs
    planes, members, width = hi_ref.shape
    rows = courant_ref.shape[0] // (2 * levels)
    cols = width // (rows - 2)
    nobs = tile_ref.shape[1]
    batches = order_ref.shape[0]
    batch = nobs // batches
    blocks = nobs // SUBLANES
    size = mine_half_ref.shape[0]

    my_lat, my_lon = lax.axis_index("lat"), lax.axis_index("lon")
    lon_even = lax.rem(my_lon, 2) == 0
    block = (join_ref.shape[0] - size) // 2
    near, far = (
        unfolded(join_ref[start : start + block, :].astype(F32)[: members // 2]) for start in (size, size + block)
    )
    west, east = jnp.where(lon_even, far, near), jnp.where(lon_even, near, far)
    halo_ref[...] = jnp.where(iota((members, LANES), 1) % 2 == 1, west, pltpu.roll(east, LANES - 1, 1))

    def complete(p, r):
        first, inner = next((a, ref) for (a, z), ref in zip(parts, inner_refs, strict=True) if a <= p < z)
        n = p * rows + r
        f = inner[p - first, r] + edge_factor(courant_ref, levels, p, r) * pltpu.roll(halo_ref[...], LANES - 1 - 2 * n, 1)
        split_store(f, hi_ref, lo_ref, p, (r - 1) * cols)

    todo = [(p, r) for p in range(planes) for r in range(1, rows - 1)]
    each = -(-len(todo) // nobs)

    me = my_lat * n_lon + my_lon
    tile = in_order(tile_ref[...], order_ref)
    bits = jnp.concatenate(
        [bits_ref[pl.ds(pl.multiple_of(order_ref[i] * batch, batch), batch), :] for i in range(batches)], axis=0
    )
    mask = tile_mask(bits, tile[:1])
    mine = tile_mask(bits, jnp.full((1, LANES), me, jnp.int32))
    mask_ref[...] = mask
    mine_ref[...] = mine
    square = jnp.concatenate([mask, jnp.zeros((LANES - nobs, LANES), F32)], axis=0)
    turned = square.T

    mine_half, other_half = mine_half_ref[...].astype(F32), join_ref[:size, :].astype(F32)
    lower = jnp.where(lon_even, mine_half, other_half)
    upper = jnp.where(lon_even, other_half, mine_half)
    payload = jnp.concatenate([lower, upper[2 * size - 2 * members - 2 * SUBLANES :]], axis=0)
    own = payload[:members]
    far = payload[members : 2 * members]
    factors = payload[2 * members :]
    both = own + far * (factors[:1] + factors[SUBLANES : SUBLANES + 1])
    prior = jnp.where(iota((members, LANES), 1) < nobs, both + pltpu.roll(both, nobs, 1), 0.0)
    mean = jnp.sum(prior, axis=0, keepdims=True) * (1.0 / members)
    spread = prior - mean
    inv = 1.0 / (members - 1)
    gram = inv * lax.dot_general(spread, spread, (((0,), (0,)), ((), ())), precision=HIGHEST, preferred_element_type=F32)
    tall = jnp.concatenate([spread, jnp.zeros((LANES - members, LANES), F32)], axis=0).T

    def cut(array):
        return [array[b * SUBLANES : (b + 1) * SUBLANES] for b in range(blocks)]

    c_rows, b_rows, a_rows = cut(gram), cut(tall * inv), cut(tall)
    turns = cut(turned)
    mean = jnp.broadcast_to(mean, (SUBLANES, LANES))
    mean_own = jnp.zeros((1, LANES), F32)

    def whole(array, s):
        return jnp.broadcast_to(array[s : s + 1], (SUBLANES, LANES))

    def lanes(array, k):
        return jnp.broadcast_to(array[:, k : k + 1], (SUBLANES, LANES))

    for b in range(blocks):
        base = b * SUBLANES
        at = order_ref[base // batch] * batch + base % batch
        ahead = range(b, min(b + 3, blocks))
        columns = {i: [lanes(c_rows[i], base + j) for j in range(SUBLANES)] for i in ahead}
        allowed = {i: [lanes(turns[i], base + j) for j in range(SUBLANES)] for i in ahead}
        place = move_ref.at[b % 2]
        for j in range(SUBLANES):
            place[4 + j] = columns[b][j]
            place[12 + j] = allowed[b][j]

        def taken(i, s):
            return jnp.broadcast_to(move_ref[b % 2, i, s : s + 1, :], (SUBLANES, LANES))

        entry = {(i, j): taken(4 + j, i) for j in range(SUBLANES) for i in range(j, SUBLANES)}
        allow = {(j, q): taken(12 + q, j) for q in range(SUBLANES) for j in range(q + 1, SUBLANES)}
        means = [lanes(mean, base + j) for j in range(SUBLANES)]
        alphas, afters = {}, {}
        for q in range(SUBLANES):
            k = base + q
            for _ in range(each):
                if todo:
                    complete(*todo.pop(0))
            r = jnp.full((SUBLANES, LANES), var_ref[at + q], F32)
            o = jnp.full((SUBLANES, LANES), value_ref[at + q], F32)
            g = entry[q, q]
            u = lax.rsqrt(total if q else g + (r + EPSILON))
            uu = u * u
            c = -uu * pl.reciprocal(1.0 + jnp.sqrt(r) * u, approx=True)
            gain = uu * (o - means[q])
            if q + 1 < SUBLANES:
                g_j, masked = entry[q + 1, q], allow[q + 1, q] * entry[q + 1, q]
                next_r = jnp.full((SUBLANES, LANES), var_ref[at + q + 1], F32) + EPSILON
                total = (entry[q + 1, q + 1] + next_r) + c * (2.0 * masked * g_j + c * (masked * masked * g))
            for j in range(q + 1, SUBLANES):
                masked = allow[j, q] * entry[j, q]
                alphas[j, q] = masked * c
                afters[j, q] = entry[j, q] + alphas[j, q] * g
                means[j] = means[j] + masked * gain
            for j in range(q + 1, SUBLANES):
                for i in range(j, SUBLANES):
                    entry[i, j] = entry[i, j] + alphas[i, q] * afters[j, q] + entry[i, q] * alphas[j, q]
            g_c, g_b, g_a = whole(c_rows[b], q), whole(b_rows[b], q), whole(a_rows[b], q)
            masked_c = jnp.broadcast_to(mask_ref[k : k + 1, :], (SUBLANES, LANES)) * g_c
            masked_b = jnp.broadcast_to(mine_ref[k : k + 1, :], (SUBLANES, LANES)) * g_b
            alpha_c, alpha_b = masked_c * c, masked_b * c
            h_c, h_b = g_c + alpha_c * g, g_b + alpha_b * g
            mean = mean + masked_c * gain
            mean_own = mean_own + (masked_b * gain)[:1]
            alpha_ref[k : k + 1, :] = alpha_b[:1]
            anomaly_ref[k : k + 1, :] = g_a[:1]
            row_ref[0, k : k + 1, :] = alpha_c[:1]
            row_ref[1, k : k + 1, :] = h_c[:1]
            row_ref[2, k : k + 1, :] = h_b[:1]
            row_ref[3, k : k + 1, :] = g_c[:1]
            for i in ahead:
                if i == b and q == SUBLANES - 1:
                    continue
                g_i = columns[i][q]
                alpha_i = allowed[i][q] * g_i * c
                c_rows[i] = c_rows[i] + alpha_i * h_c + g_i * alpha_c
                b_rows[i] = b_rows[i] + alpha_i * h_b + g_i * alpha_b
                a_rows[i] = a_rows[i] + alpha_i * g_a
                for j in range(q + 1, SUBLANES):
                    columns[i][j] = columns[i][j] + alpha_i * afters[j, q] + g_i * alphas[j, q]
        if b + 3 < blocks:
            own = slice(base, base + SUBLANES)
            alpha_c, h_c, h_b, g_c = (row_ref[i, own, :] for i in range(4))
            left = jnp.concatenate([alpha_c, g_c], axis=0)[:, :nobs]
            zero = jnp.zeros((SUBLANES, LANES), F32)
            upper = jnp.concatenate([h_c, h_b, anomaly_ref[own, :]], axis=1)
            right = jnp.concatenate([upper, jnp.concatenate([alpha_c, alpha_ref[own, :], zero], axis=1)], axis=0)
            change = lax.dot_general(left, right, (((0,), (0,)), ((), ())), precision=HIGHEST, preferred_element_type=F32)
            for i in range(b + 3, blocks):
                part = change[i * SUBLANES : (i + 1) * SUBLANES]
                c_rows[i] = c_rows[i] + part[:, :LANES]
                b_rows[i] = b_rows[i] + part[:, LANES : 2 * LANES]
                a_rows[i] = a_rows[i] + part[:, 2 * LANES :]

    transform = lax.dot_general(
        anomaly_ref[...], alpha_ref[...], (((0,), (0,)), ((), ())), precision=HIGHEST, preferred_element_type=F32
    )
    transform = transform[:members] + mean_own + (iota((members, LANES), 0) == iota((members, LANES), 1)).astype(F32)
    for item in todo:
        complete(*item)
    transform_ref[...] = transform


def analysis_kernel(n_lat, levels, parts, *refs):
    transform_ref, halo_ref, hi_ref, lo_ref, courant_ref = refs[:5]
    odd_pieces, pair_pieces = PLAN["pieces"]
    pair_refs, refs = refs[5 : 5 + pair_pieces], refs[5 + pair_pieces :]
    odd_refs, refs = refs[:odd_pieces], refs[odd_pieces:]
    inner_refs, refs = refs[: len(parts)], refs[len(parts) :]
    out_hbm, edge_hi_ref, edge_lo_ref, out_ref, wide_ref, out_sem = refs
    planes, members, width = hi_ref.shape
    rows = courant_ref.shape[0] // (2 * levels)
    cols = width // (rows - 2)
    my_lat = lax.axis_index("lat")
    lat_even = lax.rem(my_lat, 2) == 0
    has_south, has_north = (my_lat > 0).astype(F32), (my_lat < n_lat - 1).astype(F32)

    transform = transform_ref[...]
    hi = transform.astype(BF16).astype(F32)
    lo = transform - hi
    lane = iota((members, LANES), 1)
    spill = 2 * members - LANES
    left = jnp.where(lane < members, hi, pltpu.roll(lo, members, 1))
    right = jnp.where(lane < spill, pltpu.roll(lo, members, 1), pltpu.roll(hi, spill, 1))
    terms = jnp.concatenate([left, right], axis=1).astype(BF16)[:, : 3 * members]
    for p in range(planes):
        first, inner = next((a, ref) for (a, z), ref in zip(parts, inner_refs, strict=True) if a <= p < z)
        _, _, south, north = winds_of(courant_ref, levels, p)
        near, far = (
            one[p // (planes // len(one))][p % (planes // len(one))].astype(F32) for one in (pair_refs, odd_refs)
        )
        for r in (0, rows - 1):
            n = p * rows + r
            f = inner[p - first, r] + edge_factor(courant_ref, levels, p, r) * pltpu.roll(halo_ref[...], LANES - 1 - 2 * n, 1)
            if r == 0:
                f = f + (south[:1] * has_south) * jnp.where(lat_even, far, near)
            else:
                f = f + (north[r:] * has_north) * jnp.where(lat_even, near, far)
            split_store(f, edge_hi_ref, edge_lo_ref, p, 0 if r == 0 else cols)
    for p in range(planes):
        for h_ref, l_ref, which in ((hi_ref, lo_ref, range(1, rows - 1)), (edge_hi_ref, edge_lo_ref, (0, rows - 1))):
            stacked = jnp.concatenate([h_ref[p], h_ref[p], l_ref[p]], axis=0)
            result = jnp.dot(terms, stacked, preferred_element_type=F32)
            for i, r in enumerate(which):
                wide_ref[p % 2, pl.ds(r, members, stride=rows), :] = result[:, i * cols : (i + 1) * cols]
        out_ref[p] = wide_ref[p % 2].astype(BF16)
        pltpu.make_async_copy(out_ref.at[p], out_hbm.at[p], out_sem.at[p]).start()
    for p in range(planes):
        pltpu.make_async_copy(out_ref.at[p], out_hbm.at[p], out_sem.at[p]).wait()


def exchanged(x, axis, step):
    return lax.ppermute(x, axis, [(i, i ^ step) for i in range(lax.axis_size(axis))])


def exchanged_odd(x, axis):
    count = lax.axis_size(axis)
    return lax.ppermute(x, axis, [pair for i in range(1, count, 2) for pair in ((i, (i + 1) % count), ((i + 1) % count, i))])


def per_device(prior_state, courant, obs_tile, obs_site, obs_value, obs_var, loc_bits, batch_order):
    fields, levels, members, rows, cols = prior_state.shape
    planes, depth = fields * levels, members * rows
    n_lat, n_lon = lax.axis_size("lat"), lax.axis_size("lon")
    nobs = obs_tile.shape[0]
    x = prior_state.reshape(planes, depth, cols)
    winds = courant.reshape(2 * levels * rows, cols)
    tile = obs_tile.reshape(1, nobs)
    site = obs_site.reshape(1, nobs)

    arguments = [pltpu.with_memory_space_constraint(array, pltpu.HBM) for array in (x, winds, tile, site, batch_order)]
    payload = pl.pallas_call(
        functools.partial(observe_kernel, n_lon, levels),
        out_shape=jax.ShapeDtypeStruct((2 * members + 2 * SUBLANES, LANES), BF16),
        in_specs=[HBM] * 5,
        out_specs=VMEM,
        scratch_shapes=[
            pltpu.VMEM(x.shape, BF16),
            pltpu.VMEM(winds.shape, F32),
            pltpu.VMEM(tile.shape, jnp.int32),
            pltpu.VMEM(site.shape, jnp.int32),
            pltpu.SMEM(batch_order.shape, jnp.int32),
            pltpu.SemaphoreType.DMA((1,)),
            pltpu.SemaphoreType.DMA((4,)),
        ],
        compiler_params=PARAMS,
        name="observe",
    )(*arguments)
    payload, x = lax.optimization_barrier((payload, x))

    def local(kernel, name, out, scratch, *operands):
        return pl.pallas_call(
            kernel,
            out_shape=out,
            in_specs=[VMEM] * len(operands),
            out_specs=jax.tree.map(lambda _: VMEM, out),
            scratch_shapes=scratch,
            compiler_params=PARAMS,
            cost_estimate=SMALL,
            name=name,
        )(*operands)

    def edge_rows(x, facing):
        pieces = PLAN["pieces"][facing]
        return local(
            functools.partial(edge_rows_kernel, rows, facing),
            "edge_rows",
            [jax.ShapeDtypeStruct((planes // pieces, members, cols), BF16)] * pieces,
            [pltpu.VMEM((planes, depth, cols), F32)],
            x,
        )

    def inner(x, start, stop):
        return local(
            functools.partial(inner_kernel, levels, start),
            "inner",
            jax.ShapeDtypeStruct((stop - start, rows, members, cols), F32),
            [pltpu.VMEM((stop - start, depth, cols), F32), pltpu.VMEM((stop - start, 5, rows, cols), F32)],
            x,
            winds,
        )

    lat_steps = [1 << i for i in range(n_lat.bit_length() - 1)]
    lon_steps = [2 << i for i in range(n_lon.bit_length() - 2)]
    size = (payload.shape[0] // 2 + 15) // 16 * 16
    half_type = jax.ShapeDtypeStruct((size, LANES), BF16)
    done = {}
    parts, inners = [], []

    def beside(stage, x):
        if stage == PLAN["columns"]:
            done["near"], done["column"] = local(
                functools.partial(edge_columns_kernel, rows),
                "edge_columns",
                [jax.ShapeDtypeStruct(((members // 2 + 15) // 16 * 16, LANES), BF16)] * 2,
                [pltpu.VMEM((planes, depth, cols), F32)],
                x,
            )
        for name, facing, send in (
            ("pair", True, lambda part: exchanged(part, "lat", 1)),
            ("odd", False, lambda part: exchanged_odd(part, "lat")),
        ):
            if stage == PLAN[name]:
                done[name + "_rows"] = edge_rows(x, facing)
            if stage == PLAN[name + "_send"]:
                done[name] = [send(part) for part in done[name + "_rows"]]
        for start, stop in PLAN["inner"].get(stage, ()):
            parts.append((start, stop))
            inners.append(inner(x, start, stop))

    def settle(stage, *arrays):
        held = [done.pop(name) for name in PLAN["settle"].get(stage, ())]
        names = PLAN["settle"].get(stage, ())
        arrays, new, held = lax.optimization_barrier((arrays, list(inners), held))
        inners[:] = new
        done.update(zip(names, held, strict=True))
        return arrays

    other = exchanged(payload, "lon", 1)
    beside(0, x)
    half = local(half_kernel, "half", half_type, [], payload, other)
    half, x = settle(0, half, x)
    stage = 1
    for step in lat_steps:
        other = exchanged(half, "lat", step)
        beside(stage, x)
        half = half + other
        half, x = settle(stage, half, x)
        stage += 1
    block, blocks = done["column"], []
    column_rows = block.shape[0]
    for step in lon_steps:
        other = exchanged(jnp.concatenate([half, block], axis=0), "lon", step)
        beside(stage, x)
        block = other[size:]
        blocks.append(block)
        if step != lon_steps[-1]:
            half = half + other[:size]
            half, block, x = settle(stage, half, block, x)
            stage += 1
    join_type = jax.ShapeDtypeStruct((size + 2 * column_rows, LANES), BF16)
    join = local(
        functools.partial(join_kernel, n_lon, len(blocks)), "join", join_type, [], half, other, done["near"], *blocks
    )
    join, x = settle(stage, join, x)
    received = exchanged(join, "lon", 1)
    beside(stage + 1, x)

    middle_type = jax.ShapeDtypeStruct((planes, members, (rows - 2) * cols), BF16)
    square_type = jax.ShapeDtypeStruct((members, LANES), F32)
    transform, halo, hi, lo = pl.pallas_call(
        functools.partial(filter_kernel, n_lon, levels, parts),
        out_shape=[square_type, square_type, middle_type, middle_type],
        in_specs=[SMEM] * 3 + [VMEM] * (5 + len(parts)),
        out_specs=[VMEM] * 4,
        scratch_shapes=[pltpu.VMEM((nobs, LANES), F32)] * 4 + [pltpu.VMEM((4, nobs, LANES), F32), pltpu.VMEM((2, 32, SUBLANES, LANES), F32)],
        compiler_params=PARAMS,
        cost_estimate=pl.CostEstimate(flops=PLAN["filter"], bytes_accessed=0, transcendentals=0),
        name="filter",
    )(batch_order, obs_value, obs_var, join[:size], received, tile, loc_bits, winds, *inners)

    edge_type = pltpu.VMEM((planes, members, 2 * cols), BF16)
    out = pl.pallas_call(
        functools.partial(analysis_kernel, n_lat, levels, parts),
        out_shape=jax.ShapeDtypeStruct((planes, depth, cols), BF16),
        in_specs=[VMEM] * (5 + sum(PLAN["pieces"]) + len(parts)),
        out_specs=HBM,
        scratch_shapes=[
            edge_type,
            edge_type,
            pltpu.VMEM((planes, depth, cols), BF16),
            pltpu.VMEM((2, depth, cols), F32),
            pltpu.SemaphoreType.DMA((planes,)),
        ],
        compiler_params=PARAMS,
        name="analysis",
    )(transform, halo, hi, lo, winds, *done["pair"], *done["odd"], *inners)
    return out.reshape(prior_state.shape)


def solution(mesh):
    placed = (P(None, None, None, "lat", "lon"), P(None, None, "lat", "lon")) + (P(),) * 6
    return jax.shard_map(
        per_device,
        mesh=mesh,
        in_specs=placed,
        out_specs=P(None, None, None, "lat", "lon"),
        check_vma=False,
    )
```

```python
import functools

import jax
import jax.numpy as jnp
from jax import lax
from jax.experimental import pallas as pl
from jax.experimental.pallas import tpu as pltpu
from jax.sharding import PartitionSpec as P

EPSILON = 1e-05
HIGHEST = lax.Precision.HIGHEST
LANES = 128
PLAN = {"filter": 1000000000, "columns": 0, "pieces": (1, 1), "pair": 2, "pair_send": 2, "odd": 2, "odd_send": 4, "inner": {1: [(0, 5)], 2: [(5, 8)]}, "settle": {0: ["column"], 2: ["pair_rows", "odd_rows"], 3: ["odd_rows"], 4: ["pair"]}}
SUBLANES = 8
F32 = jnp.float32
BF16 = jnp.bfloat16
VMEM = pl.BlockSpec(memory_space=pltpu.VMEM)
SMEM = pl.BlockSpec(memory_space=pltpu.SMEM)
HBM = pl.BlockSpec(memory_space=pltpu.HBM)
SMALL = pl.CostEstimate(flops=0, bytes_accessed=0, transcendentals=0)
PARAMS = pltpu.CompilerParams(vmem_limit_bytes=16 * 1024 * 1024)


def iota(shape, dim):
    return lax.broadcasted_iota(jnp.int32, shape, dim)


def in_order(row, order_ref):
    nobs = row.shape[1]
    batches = order_ref.shape[0]
    batch = nobs // batches
    wide = jnp.concatenate([row, jnp.zeros((1, LANES - nobs), row.dtype)], axis=1)
    wide = jnp.broadcast_to(wide, (SUBLANES, LANES))
    lane = iota((SUBLANES, LANES), 1)
    result = jnp.zeros_like(wide)
    for i in range(batches):
        moved = pltpu.roll(wide, lax.rem(i * batch - order_ref[i] * batch + LANES, LANES), 1)
        result = jnp.where(lane // batch == i, moved, result)
    return result


def observe_kernel(
    n_lon, levels, x_hbm, courant_hbm, tile_hbm, site_hbm, order_hbm, pay_ref, x_ref, courant_ref, tile_ref, site_ref, order_ref, x_sem, sem
):
    planes, depth, cols = x_ref.shape
    small = [
        pltpu.make_async_copy(source, target, sem.at[i])
        for i, (source, target) in enumerate(
            ((order_hbm, order_ref), (tile_hbm, tile_ref), (site_hbm, site_ref), (courant_hbm, courant_ref))
        )
    ]
    for copy in small:
        copy.start()
    pieces = x_sem.shape[0]
    share = planes // pieces
    large = [
        pltpu.make_async_copy(x_hbm.at[i * share : (i + 1) * share], x_ref.at[i * share : (i + 1) * share], x_sem.at[i])
        for i in range(pieces)
    ]
    for copy in large:
        copy.start()
    for copy in small[:3]:
        copy.wait()
    rows = courant_ref.shape[0] // (2 * levels)
    members = depth // rows
    nobs = tile_ref.shape[1]
    cells = rows * cols
    my_lat, my_lon = lax.axis_index("lat"), lax.axis_index("lon")
    me = my_lat * n_lon + my_lon

    tile = in_order(tile_ref[...], order_ref)
    site = in_order(site_ref[...], order_ref)
    tile = tile + pltpu.roll(tile, nobs, 1)
    site = site + pltpu.roll(site, nobs, 1)
    shape = (SUBLANES, LANES)
    lane = iota(shape, 1)
    sub = iota(shape, 0)
    first = lane < nobs
    plane = site // cells
    row = (site // cols) % rows
    col = site % cols
    level = plane % levels
    lat, lon = tile // n_lon, tile % n_lon
    owner = tile == me
    from_west = (lat == my_lat) & ((lon + n_lon - 1) % n_lon == my_lon) & (col == 0)
    from_east = (lat == my_lat) & ((lon + 1) % n_lon == my_lon) & (col == cols - 1)
    from_south = (lat - 1 == my_lat) & (lon == my_lon) & (row == 0)
    from_north = (lat + 1 == my_lat) & (lon == my_lon) & (row == rows - 1)
    beside = from_west | from_east
    above = from_south | from_north
    far_col = jnp.where(from_west, cols - 1, jnp.where(from_east, 0, jnp.where(above, col, -1)))
    far_row = jnp.where(from_south, rows - 1, jnp.where(from_north, 0, row))

    small[3].wait()
    down = iota((cols, LANES), 0)
    picked = jnp.dot(
        courant_ref[...], (down == col[:1]).astype(F32), precision=HIGHEST, preferred_element_type=F32
    )
    which = iota((2 * levels * rows, LANES), 0)
    at_cell = (level * rows + row)[:1]
    cu = jnp.sum(jnp.where(which == at_cell, picked, 0.0), axis=0, keepdims=True)
    cv = jnp.sum(jnp.where(which == at_cell + levels * rows, picked, 0.0), axis=0, keepdims=True)
    west, east = jnp.maximum(cu, 0.0), -jnp.minimum(cu, 0.0)
    south, north = jnp.maximum(cv, 0.0), -jnp.minimum(cv, 0.0)
    centre = 1.0 - west - east - south - north

    zero = jnp.zeros(shape, F32)
    own_rows = jnp.where(sub == row, centre, zero)
    own_rows = jnp.where(sub == row - 1, south, own_rows)
    own_rows = jnp.where(sub == row + 1, north, own_rows)
    half0 = jnp.where(first, own_rows, jnp.where(sub == row, west, zero))
    half0 = jnp.where(owner, half0, zero)
    half1 = jnp.where(first, jnp.where(owner & (sub == row), east, zero), ((beside | above) & (sub == far_row)).astype(F32))
    col0 = jnp.where(first, col, jnp.where(col > 0, col - 1, -1))
    col1 = jnp.where(first, jnp.where(col < cols - 1, col + 1, -1), far_col)
    at = jnp.concatenate([jnp.where(c < 0, -1, plane * cols + c)[:1] for c in (col0, col1)], axis=1)
    picks = (iota((planes * cols, 2 * LANES), 0) == at).astype(F32).astype(BF16)
    weights = jnp.concatenate([half0, half1], axis=1)
    values = None
    for i in range(pieces):
        large[i].wait()
        block = jnp.concatenate([x_ref[p] for p in range(i * share, (i + 1) * share)], axis=1)
        part = jnp.dot(block, picks[i * share * cols : (i + 1) * share * cols], preferred_element_type=F32)
        values = part if values is None else values + part
    values = values.reshape(members, rows, 2 * LANES)
    both = jnp.sum(values * weights[None], axis=1)
    low, high = both[:, :LANES], both[:, LANES:]
    lane_m = iota((members, LANES), 1)
    own = jnp.where(lane_m < nobs, low + pltpu.roll(low, nobs, 1) + high, 0.0)
    far = jnp.where(lane_m < nobs, 0.0, high)
    put_split(pay_ref, 0, own, nobs)
    along_lon = pltpu.roll(jnp.where(beside[:1], far, 0.0), nobs, 1)
    pay_ref[members : 2 * members, :] = (along_lon + jnp.where(above[:1], far, 0.0)).astype(BF16)
    factor_lon = jnp.where(col == 0, west, jnp.where(col == cols - 1, east, zero))
    factor_lat = jnp.where(row == 0, south, jnp.where(row == rows - 1, north, zero))
    factors = jnp.where(owner, jnp.where(first, factor_lon, factor_lat), zero)
    coarse = factors.astype(BF16)
    fine = (factors - coarse.astype(F32)).astype(BF16)
    pay_ref[2 * members :, :] = jnp.concatenate([coarse, fine], axis=0)


def put_split(ref, start, values, nobs):
    coarse = values.astype(BF16)
    fine = (values - coarse.astype(F32)).astype(BF16)
    both = coarse.astype(F32) + pltpu.roll(fine.astype(F32), nobs, 1)
    ref[start : start + values.shape[0], :] = both.astype(BF16)


def edge_rows_kernel(rows, facing, x_ref, *refs):
    planes, depth, cols = x_ref.shape
    members = depth // rows
    upper = lax.rem(lax.axis_index("lat"), 2) == (0 if facing else 1)
    row = jnp.where(upper, rows - 1, 0)
    *row_refs, wide_ref = refs
    share = planes // len(row_refs)
    for p in range(planes):
        wide_ref[p] = x_ref[p].astype(F32)
        row_refs[p // share][p % share] = wide_ref[p, pl.ds(row, members, stride=rows), :].astype(BF16)


def folded(values, size):
    half = values.shape[0] // 2
    odd = iota((half, LANES), 1) % 2 == 1
    both = jnp.where(odd, values[:half], pltpu.roll(values[half:], LANES - 1, 1))
    return jnp.concatenate([both, jnp.zeros((size - half, LANES), F32)], axis=0)


def unfolded(values):
    return jnp.concatenate([values, pltpu.roll(values, 1, 1)], axis=0)


def edge_columns_kernel(rows, x_ref, near_ref, far_ref, wide_ref):
    planes, depth, cols = x_ref.shape
    members = depth // rows
    lane = iota((members, LANES), 1)
    total = jnp.zeros((members, LANES), F32)
    for p in range(planes):
        wide_ref[p] = x_ref[p].astype(F32)
        for r in range(rows):
            n = p * rows + r
            cell = wide_ref[p, pl.ds(r, members, stride=rows), :]
            total = jnp.where(lane // 2 == n, pltpu.roll(cell, 2 * n + 1, 1) if 2 * n + 1 < LANES else cell, total)
    last = pltpu.roll(total, 1, 1)
    even = lax.rem(lax.axis_index("lon"), 2) == 0
    size = near_ref.shape[0]
    near_ref[...] = folded(jnp.where(even, last, total), size).astype(BF16)
    far_ref[...] = folded(jnp.where(even, total, last), size).astype(BF16)


def winds_of(courant_ref, levels, p):
    rows = courant_ref.shape[0] // (2 * levels)
    level = p % levels
    cu = courant_ref[level * rows : (level + 1) * rows, :]
    cv = courant_ref[(levels + level) * rows : (levels + level + 1) * rows, :]
    return jnp.maximum(cu, 0.0), -jnp.minimum(cu, 0.0), jnp.maximum(cv, 0.0), -jnp.minimum(cv, 0.0)


def inner_kernel(levels, start, x_ref, courant_ref, inner_ref, wide_ref, factor_ref):
    planes, rows, members, cols = inner_ref.shape
    lane = iota((rows, cols), 1)
    for i in range(planes):
        p = start + i
        wide_ref[i] = x_ref[p].astype(F32)
        west, east, south, north = winds_of(courant_ref, levels, p)
        factor_ref[i, 0] = 1.0 - west - east - south - north
        factor_ref[i, 1] = jnp.where(lane == 0, 0.0, west)
        factor_ref[i, 2] = jnp.where(lane == cols - 1, 0.0, east)
        factor_ref[i, 3] = south
        factor_ref[i, 4] = north
        for m in range(0, members, SUBLANES):
            cells = [wide_ref[i, pl.ds(m * rows + r, SUBLANES, stride=rows), :] for r in range(rows)]
            for r in range(rows):
                x = cells[r]
                value = factor_ref[i, 0, r : r + 1, :] * x
                value = value + factor_ref[i, 1, r : r + 1, :] * pltpu.roll(x, 1, 1)
                value = value + factor_ref[i, 2, r : r + 1, :] * pltpu.roll(x, cols - 1, 1)
                if r > 0:
                    value = value + factor_ref[i, 3, r : r + 1, :] * cells[r - 1]
                if r < rows - 1:
                    value = value + factor_ref[i, 4, r : r + 1, :] * cells[r + 1]
                inner_ref[i, r, m : m + SUBLANES, :] = value


def tile_mask(bits, tiles):
    words = bits.shape[1]
    word = tiles // 30
    place = tiles % 30
    chosen = jnp.zeros((bits.shape[0], LANES), jnp.int32)
    for w in range(words):
        chosen = jnp.where(word == w, bits[:, w : w + 1], chosen)
    return (jnp.right_shift(chosen, place) & 1).astype(F32)


def half_kernel(full_ref, other_ref, half_ref):
    size = half_ref.shape[0]
    upper = lax.rem(lax.axis_index("lon"), 2) == 1
    total = full_ref[...].astype(F32) + other_ref[...].astype(F32)
    half_ref[...] = jnp.where(upper, total[total.shape[0] - size :], total[:size]).astype(BF16)


def join_kernel(n_lon, stages, *refs):
    own_ref, other_ref, column_ref = refs[:3]
    column_refs, out_ref = refs[3 : 3 + stages], refs[-1]
    size, block = own_ref.shape[0], column_ref.shape[0]
    other_lon = lax.bitwise_xor(lax.axis_index("lon"), 1)
    odd = jnp.where(lax.rem(other_lon, 2) == 0, lax.rem(other_lon + n_lon - 1, n_lon), other_lon)
    far = column_refs[0][...].astype(F32)
    for i in range(1, stages):
        low = (2 << i) - 1
        far = jnp.where(jnp.bitwise_and(odd, low) == low, column_refs[i][...].astype(F32), far)
    out_ref[:size, :] = (own_ref[...].astype(F32) + other_ref[:size, :].astype(F32)).astype(BF16)
    out_ref[size : size + block, :] = column_ref[...]
    out_ref[size + block :, :] = far.astype(BF16)


def split_store(f, hi_ref, lo_ref, p, start):
    cols = f.shape[1]
    hi = f.astype(BF16)
    hi_ref[p, :, start : start + cols] = hi
    lo_ref[p, :, start : start + cols] = (f - hi.astype(F32)).astype(BF16)


def edge_factor(courant_ref, levels, p, r):
    rows, cols = courant_ref.shape[0] // (2 * levels), courant_ref.shape[1]
    west, east, _, _ = winds_of(courant_ref, levels, p)
    lane = iota((rows, cols), 1)
    return jnp.where(lane == 0, west, jnp.where(lane == cols - 1, east, 0.0))[r : r + 1]


def filter_kernel(n_lon, levels, parts, *refs):
    order_ref, value_ref, var_ref, mine_half_ref, join_ref, tile_ref, bits_ref, courant_ref = refs[:8]
    inner_refs, refs = refs[8 : 8 + len(parts)], refs[8 + len(parts) :]
    transform_ref, halo_ref, hi_ref, lo_ref, alpha_ref, anomaly_ref, mask_ref, mine_ref, row_ref, move_ref = refs
    planes, members, width = hi_ref.shape
    rows = courant_ref.shape[0] // (2 * levels)
    cols = width // (rows - 2)
    nobs = tile_ref.shape[1]
    batches = order_ref.shape[0]
    batch = nobs // batches
    blocks = nobs // SUBLANES
    size = mine_half_ref.shape[0]

    my_lat, my_lon = lax.axis_index("lat"), lax.axis_index("lon")
    lon_even = lax.rem(my_lon, 2) == 0
    block = (join_ref.shape[0] - size) // 2
    near, far = (
        unfolded(join_ref[start : start + block, :].astype(F32)[: members // 2]) for start in (size, size + block)
    )
    west, east = jnp.where(lon_even, far, near), jnp.where(lon_even, near, far)
    halo_ref[...] = jnp.where(iota((members, LANES), 1) % 2 == 1, west, pltpu.roll(east, LANES - 1, 1))

    def complete(p, r):
        first, inner = next((a, ref) for (a, z), ref in zip(parts, inner_refs, strict=True) if a <= p < z)
        n = p * rows + r
        f = inner[p - first, r] + edge_factor(courant_ref, levels, p, r) * pltpu.roll(halo_ref[...], LANES - 1 - 2 * n, 1)
        split_store(f, hi_ref, lo_ref, p, (r - 1) * cols)

    todo = [(p, r) for p in range(planes) for r in range(1, rows - 1)]
    each = -(-len(todo) // nobs)

    me = my_lat * n_lon + my_lon
    tile = in_order(tile_ref[...], order_ref)
    bits = jnp.concatenate(
        [bits_ref[pl.ds(pl.multiple_of(order_ref[i] * batch, batch), batch), :] for i in range(batches)], axis=0
    )
    mask = tile_mask(bits, tile[:1])
    mine = tile_mask(bits, jnp.full((1, LANES), me, jnp.int32))
    mask_ref[...] = mask
    mine_ref[...] = mine
    square = jnp.concatenate([mask, jnp.zeros((LANES - nobs, LANES), F32)], axis=0)
    turned = square.T

    mine_half, other_half = mine_half_ref[...].astype(F32), join_ref[:size, :].astype(F32)
    lower = jnp.where(lon_even, mine_half, other_half)
    upper = jnp.where(lon_even, other_half, mine_half)
    payload = jnp.concatenate([lower, upper[2 * size - 2 * members - 2 * SUBLANES :]], axis=0)
    own = payload[:members]
    far = payload[members : 2 * members]
    factors = payload[2 * members :]
    both = own + far * (factors[:1] + factors[SUBLANES : SUBLANES + 1])
    prior = jnp.where(iota((members, LANES), 1) < nobs, both + pltpu.roll(both, nobs, 1), 0.0)
    mean = jnp.sum(prior, axis=0, keepdims=True) * (1.0 / members)
    spread = prior - mean
    inv = 1.0 / (members - 1)
    gram = inv * lax.dot_general(spread, spread, (((0,), (0,)), ((), ())), precision=HIGHEST, preferred_element_type=F32)
    tall = jnp.concatenate([spread, jnp.zeros((LANES - members, LANES), F32)], axis=0).T

    def cut(array):
        return [array[b * SUBLANES : (b + 1) * SUBLANES] for b in range(blocks)]

    c_rows, b_rows, a_rows = cut(gram), cut(tall * inv), cut(tall)
    turns = cut(turned)
    mean = jnp.broadcast_to(mean, (SUBLANES, LANES))
    mean_own = jnp.zeros((1, LANES), F32)

    def whole(array, s):
        return jnp.broadcast_to(array[s : s + 1], (SUBLANES, LANES))

    def lanes(array, k):
        return jnp.broadcast_to(array[:, k : k + 1], (SUBLANES, LANES))

    for b in range(blocks):
        base = b * SUBLANES
        at = order_ref[base // batch] * batch + base % batch
        ahead = range(b, min(b + 3, blocks))
        columns = {i: [lanes(c_rows[i], base + j) for j in range(SUBLANES)] for i in ahead}
        allowed = {i: [lanes(turns[i], base + j) for j in range(SUBLANES)] for i in ahead}
        place = move_ref.at[b % 2]
        for j in range(SUBLANES):
            place[4 + j] = columns[b][j]
            place[12 + j] = allowed[b][j]

        def taken(i, s):
            return jnp.broadcast_to(move_ref[b % 2, i, s : s + 1, :], (SUBLANES, LANES))

        entry = {(i, j): taken(4 + j, i) for j in range(SUBLANES) for i in range(j, SUBLANES)}
        allow = {(j, q): taken(12 + q, j) for q in range(SUBLANES) for j in range(q + 1, SUBLANES)}
        means = [lanes(mean, base + j) for j in range(SUBLANES)]
        alphas, afters = {}, {}
        for q in range(SUBLANES):
            k = base + q
            for _ in range(each):
                if todo:
                    complete(*todo.pop(0))
            r = jnp.full((SUBLANES, LANES), var_ref[at + q], F32)
            o = jnp.full((SUBLANES, LANES), value_ref[at + q], F32)
            g = entry[q, q]
            u = lax.rsqrt(total if q else g + (r + EPSILON))
            uu = u * u
            c = -uu * pl.reciprocal(1.0 + jnp.sqrt(r) * u, approx=True)
            gain = uu * (o - means[q])
            if q + 1 < SUBLANES:
                g_j, masked = entry[q + 1, q], allow[q + 1, q] * entry[q + 1, q]
                next_r = jnp.full((SUBLANES, LANES), var_ref[at + q + 1], F32) + EPSILON
                total = (entry[q + 1, q + 1] + next_r) + c * (2.0 * masked * g_j + c * (masked * masked * g))
            for j in range(q + 1, SUBLANES):
                masked = allow[j, q] * entry[j, q]
                alphas[j, q] = masked * c
                afters[j, q] = entry[j, q] + alphas[j, q] * g
                means[j] = means[j] + masked * gain
            for j in range(q + 1, SUBLANES):
                for i in range(j, SUBLANES):
                    entry[i, j] = entry[i, j] + alphas[i, q] * afters[j, q] + entry[i, q] * alphas[j, q]
            g_c, g_b, g_a = whole(c_rows[b], q), whole(b_rows[b], q), whole(a_rows[b], q)
            masked_c = jnp.broadcast_to(mask_ref[k : k + 1, :], (SUBLANES, LANES)) * g_c
            masked_b = jnp.broadcast_to(mine_ref[k : k + 1, :], (SUBLANES, LANES)) * g_b
            alpha_c, alpha_b = masked_c * c, masked_b * c
            h_c, h_b = g_c + alpha_c * g, g_b + alpha_b * g
            mean = mean + masked_c * gain
            mean_own = mean_own + (masked_b * gain)[:1]
            alpha_ref[k : k + 1, :] = alpha_b[:1]
            anomaly_ref[k : k + 1, :] = g_a[:1]
            row_ref[0, k : k + 1, :] = alpha_c[:1]
            row_ref[1, k : k + 1, :] = h_c[:1]
            row_ref[2, k : k + 1, :] = h_b[:1]
            row_ref[3, k : k + 1, :] = g_c[:1]
            for i in ahead:
                if i == b and q == SUBLANES - 1:
                    continue
                g_i = columns[i][q]
                alpha_i = allowed[i][q] * g_i * c
                c_rows[i] = c_rows[i] + alpha_i * h_c + g_i * alpha_c
                b_rows[i] = b_rows[i] + alpha_i * h_b + g_i * alpha_b
                a_rows[i] = a_rows[i] + alpha_i * g_a
                for j in range(q + 1, SUBLANES):
                    columns[i][j] = columns[i][j] + alpha_i * afters[j, q] + g_i * alphas[j, q]
        if b + 3 < blocks:
            own = slice(base, base + SUBLANES)
            alpha_c, h_c, h_b, g_c = (row_ref[i, own, :] for i in range(4))
            left = jnp.concatenate([alpha_c, g_c], axis=0)[:, :nobs]
            zero = jnp.zeros((SUBLANES, LANES), F32)
            upper = jnp.concatenate([h_c, h_b, anomaly_ref[own, :]], axis=1)
            right = jnp.concatenate([upper, jnp.concatenate([alpha_c, alpha_ref[own, :], zero], axis=1)], axis=0)
            change = lax.dot_general(left, right, (((0,), (0,)), ((), ())), precision=HIGHEST, preferred_element_type=F32)
            for i in range(b + 3, blocks):
                part = change[i * SUBLANES : (i + 1) * SUBLANES]
                c_rows[i] = c_rows[i] + part[:, :LANES]
                b_rows[i] = b_rows[i] + part[:, LANES : 2 * LANES]
                a_rows[i] = a_rows[i] + part[:, 2 * LANES :]

    transform = lax.dot_general(
        anomaly_ref[...], alpha_ref[...], (((0,), (0,)), ((), ())), precision=HIGHEST, preferred_element_type=F32
    )
    transform = transform[:members] + mean_own + (iota((members, LANES), 0) == iota((members, LANES), 1)).astype(F32)
    for item in todo:
        complete(*item)
    transform_ref[...] = transform


def analysis_kernel(n_lat, levels, parts, *refs):
    transform_ref, halo_ref, hi_ref, lo_ref, courant_ref = refs[:5]
    odd_pieces, pair_pieces = PLAN["pieces"]
    pair_refs, refs = refs[5 : 5 + pair_pieces], refs[5 + pair_pieces :]
    odd_refs, refs = refs[:odd_pieces], refs[odd_pieces:]
    inner_refs, refs = refs[: len(parts)], refs[len(parts) :]
    out_hbm, edge_hi_ref, edge_lo_ref, out_ref, wide_ref, out_sem = refs
    planes, members, width = hi_ref.shape
    rows = courant_ref.shape[0] // (2 * levels)
    cols = width // (rows - 2)
    my_lat = lax.axis_index("lat")
    lat_even = lax.rem(my_lat, 2) == 0
    has_south, has_north = (my_lat > 0).astype(F32), (my_lat < n_lat - 1).astype(F32)

    transform = transform_ref[...]
    hi = transform.astype(BF16).astype(F32)
    lo = transform - hi
    lane = iota((members, LANES), 1)
    spill = 2 * members - LANES
    left = jnp.where(lane < members, hi, pltpu.roll(lo, members, 1))
    right = jnp.where(lane < spill, pltpu.roll(lo, members, 1), pltpu.roll(hi, spill, 1))
    terms = jnp.concatenate([left, right], axis=1).astype(BF16)[:, : 3 * members]
    for p in range(planes):
        first, inner = next((a, ref) for (a, z), ref in zip(parts, inner_refs, strict=True) if a <= p < z)
        _, _, south, north = winds_of(courant_ref, levels, p)
        near, far = (
            one[p // (planes // len(one))][p % (planes // len(one))].astype(F32) for one in (pair_refs, odd_refs)
        )
        for r in (0, rows - 1):
            n = p * rows + r
            f = inner[p - first, r] + edge_factor(courant_ref, levels, p, r) * pltpu.roll(halo_ref[...], LANES - 1 - 2 * n, 1)
            if r == 0:
                f = f + (south[:1] * has_south) * jnp.where(lat_even, far, near)
            else:
                f = f + (north[r:] * has_north) * jnp.where(lat_even, near, far)
            split_store(f, edge_hi_ref, edge_lo_ref, p, 0 if r == 0 else cols)
        for h_ref, l_ref, which in ((hi_ref, lo_ref, range(1, rows - 1)), (edge_hi_ref, edge_lo_ref, (0, rows - 1))):
            stacked = jnp.concatenate([h_ref[p], h_ref[p], l_ref[p]], axis=0)
            result = jnp.dot(terms, stacked, preferred_element_type=F32)
            for i, r in enumerate(which):
                wide_ref[p, pl.ds(r, members, stride=rows), :] = result[:, i * cols : (i + 1) * cols]
        out_ref[p] = wide_ref[p].astype(BF16)
        pltpu.make_async_copy(out_ref.at[p], out_hbm.at[p], out_sem.at[p]).start()
    for p in range(planes):
        pltpu.make_async_copy(out_ref.at[p], out_hbm.at[p], out_sem.at[p]).wait()


def exchanged(x, axis, step):
    return lax.ppermute(x, axis, [(i, i ^ step) for i in range(lax.axis_size(axis))])


def exchanged_odd(x, axis):
    count = lax.axis_size(axis)
    return lax.ppermute(x, axis, [pair for i in range(1, count, 2) for pair in ((i, (i + 1) % count), ((i + 1) % count, i))])


def per_device(prior_state, courant, obs_tile, obs_site, obs_value, obs_var, loc_bits, batch_order):
    fields, levels, members, rows, cols = prior_state.shape
    planes, depth = fields * levels, members * rows
    n_lat, n_lon = lax.axis_size("lat"), lax.axis_size("lon")
    nobs = obs_tile.shape[0]
    x = prior_state.reshape(planes, depth, cols)
    winds = courant.reshape(2 * levels * rows, cols)
    tile = obs_tile.reshape(1, nobs)
    site = obs_site.reshape(1, nobs)

    arguments = [pltpu.with_memory_space_constraint(array, pltpu.HBM) for array in (x, winds, tile, site, batch_order)]
    payload = pl.pallas_call(
        functools.partial(observe_kernel, n_lon, levels),
        out_shape=jax.ShapeDtypeStruct((2 * members + 2 * SUBLANES, LANES), BF16),
        in_specs=[HBM] * 5,
        out_specs=VMEM,
        scratch_shapes=[
            pltpu.VMEM(x.shape, BF16),
            pltpu.VMEM(winds.shape, F32),
            pltpu.VMEM(tile.shape, jnp.int32),
            pltpu.VMEM(site.shape, jnp.int32),
            pltpu.SMEM(batch_order.shape, jnp.int32),
            pltpu.SemaphoreType.DMA((1,)),
            pltpu.SemaphoreType.DMA((4,)),
        ],
        compiler_params=PARAMS,
        name="observe",
    )(*arguments)
    payload, x = lax.optimization_barrier((payload, x))

    def local(kernel, name, out, scratch, *operands):
        return pl.pallas_call(
            kernel,
            out_shape=out,
            in_specs=[VMEM] * len(operands),
            out_specs=jax.tree.map(lambda _: VMEM, out),
            scratch_shapes=scratch,
            compiler_params=PARAMS,
            cost_estimate=SMALL,
            name=name,
        )(*operands)

    def edge_rows(x, facing):
        pieces = PLAN["pieces"][facing]
        return local(
            functools.partial(edge_rows_kernel, rows, facing),
            "edge_rows",
            [jax.ShapeDtypeStruct((planes // pieces, members, cols), BF16)] * pieces,
            [pltpu.VMEM((planes, depth, cols), F32)],
            x,
        )

    def inner(x, start, stop):
        return local(
            functools.partial(inner_kernel, levels, start),
            "inner",
            jax.ShapeDtypeStruct((stop - start, rows, members, cols), F32),
            [pltpu.VMEM((stop - start, depth, cols), F32), pltpu.VMEM((stop - start, 5, rows, cols), F32)],
            x,
            winds,
        )

    lat_steps = [1 << i for i in range(n_lat.bit_length() - 1)]
    lon_steps = [2 << i for i in range(n_lon.bit_length() - 2)]
    size = (payload.shape[0] // 2 + 15) // 16 * 16
    half_type = jax.ShapeDtypeStruct((size, LANES), BF16)
    done = {}
    parts, inners = [], []

    def beside(stage, x):
        if stage == PLAN["columns"]:
            done["near"], done["column"] = local(
                functools.partial(edge_columns_kernel, rows),
                "edge_columns",
                [jax.ShapeDtypeStruct(((members // 2 + 15) // 16 * 16, LANES), BF16)] * 2,
                [pltpu.VMEM((planes, depth, cols), F32)],
                x,
            )
        for name, facing, send in (
            ("pair", True, lambda part: exchanged(part, "lat", 1)),
            ("odd", False, lambda part: exchanged_odd(part, "lat")),
        ):
            if stage == PLAN[name]:
                done[name + "_rows"] = edge_rows(x, facing)
            if stage == PLAN[name + "_send"]:
                done[name] = [send(part) for part in done[name + "_rows"]]
        for start, stop in PLAN["inner"].get(stage, ()):
            parts.append((start, stop))
            inners.append(inner(x, start, stop))

    def settle(stage, *arrays):
        held = [done.pop(name) for name in PLAN["settle"].get(stage, ())]
        names = PLAN["settle"].get(stage, ())
        arrays, new, held = lax.optimization_barrier((arrays, list(inners), held))
        inners[:] = new
        done.update(zip(names, held, strict=True))
        return arrays

    other = exchanged(payload, "lon", 1)
    beside(0, x)
    half = local(half_kernel, "half", half_type, [], payload, other)
    half, x = settle(0, half, x)
    stage = 1
    for step in lat_steps:
        other = exchanged(half, "lat", step)
        beside(stage, x)
        half = half + other
        half, x = settle(stage, half, x)
        stage += 1
    block, blocks = done["column"], []
    column_rows = block.shape[0]
    for step in lon_steps:
        other = exchanged(jnp.concatenate([half, block], axis=0), "lon", step)
        beside(stage, x)
        block = other[size:]
        blocks.append(block)
        if step != lon_steps[-1]:
            half = half + other[:size]
            half, block, x = settle(stage, half, block, x)
            stage += 1
    join_type = jax.ShapeDtypeStruct((size + 2 * column_rows, LANES), BF16)
    join = local(
        functools.partial(join_kernel, n_lon, len(blocks)), "join", join_type, [], half, other, done["near"], *blocks
    )
    join, x = settle(stage, join, x)
    received = exchanged(join, "lon", 1)
    beside(stage + 1, x)

    middle_type = jax.ShapeDtypeStruct((planes, members, (rows - 2) * cols), BF16)
    square_type = jax.ShapeDtypeStruct((members, LANES), F32)
    transform, halo, hi, lo = pl.pallas_call(
        functools.partial(filter_kernel, n_lon, levels, parts),
        out_shape=[square_type, square_type, middle_type, middle_type],
        in_specs=[SMEM] * 3 + [VMEM] * (5 + len(parts)),
        out_specs=[VMEM] * 4,
        scratch_shapes=[pltpu.VMEM((nobs, LANES), F32)] * 4 + [pltpu.VMEM((4, nobs, LANES), F32), pltpu.VMEM((2, 32, SUBLANES, LANES), F32)],
        compiler_params=PARAMS,
        cost_estimate=pl.CostEstimate(flops=PLAN["filter"], bytes_accessed=0, transcendentals=0),
        name="filter",
    )(batch_order, obs_value, obs_var, join[:size], received, tile, loc_bits, winds, *inners)

    edge_type = pltpu.VMEM((planes, members, 2 * cols), BF16)
    out = pl.pallas_call(
        functools.partial(analysis_kernel, n_lat, levels, parts),
        out_shape=jax.ShapeDtypeStruct((planes, depth, cols), BF16),
        in_specs=[VMEM] * (5 + sum(PLAN["pieces"]) + len(parts)),
        out_specs=HBM,
        scratch_shapes=[
            edge_type,
            edge_type,
            pltpu.VMEM((planes, depth, cols), BF16),
            pltpu.VMEM((planes, depth, cols), F32),
            pltpu.SemaphoreType.DMA((planes,)),
        ],
        compiler_params=PARAMS,
        name="analysis",
    )(transform, halo, hi, lo, winds, *done["pair"], *done["odd"], *inners)
    return out.reshape(prior_state.shape)


def solution(mesh):
    placed = (P(None, None, None, "lat", "lon"), P(None, None, "lat", "lon")) + (P(),) * 6
    return jax.shard_map(
        per_device,
        mesh=mesh,
        in_specs=placed,
        out_specs=P(None, None, None, "lat", "lon"),
        check_vma=False,
    )
```
